256 devices in a mesh: chord: 32 (over z, x), span: 8 (over y, core).
Axes of the slice: x: 4, y: 4, z: 8, core: 2. Of those that a mesh axis runs over, the one named last changes fastest.
Arguments:
- residual: float32 [5, 4, 1024, 1024], P(None, None, 'chord', 'span'), may hold values from -6 to 6
- pivot_inverse: bfloat16 [5, 5, 4, 1024, 1024], P(None, None, None, 'chord', 'span'), may hold values from -0.15 to 2, as said below
- lower_coupling: bfloat16 [5, 5, 4, 1024, 1024], P(None, None, None, 'chord', 'span'), may hold values from -1 to 0.025, as said below
- upper_coupling: bfloat16 [5, 5, 4, 1024, 1024], P(None, None, None, 'chord', 'span'), may hold values from -1 to 0.025, as said below
- span_pivot: float32 [5, 4, 1024, 1024], P(None, None, 'chord', 'span'), may hold values from 0.5 to 2
- span_lower: float32 [5, 4, 1024, 1024], P(None, None, 'chord', 'span'), may hold values from -1 to -0.8
- span_upper: float32 [5, 4, 1024, 1024], P(None, None, 'chord', 'span'), may hold values from -1 to -0.8
- normal_pivot: bfloat16 [5, 4, 1024, 1024], P(None, None, 'chord', 'span'), may hold values from 0.5 to 2
- normal_lower: bfloat16 [5, 4, 1024, 1024], P(None, None, 'chord', 'span'), may hold values from -0.8984375 to -0.19921875
- normal_upper: bfloat16 [5, 4, 1024, 1024], P(None, None, 'chord', 'span'), may hold values from -0.84765625 to -0.25
Outputs:
- update: float32 [5, 4, 1024, 1024], P(None, None, 'chord', 'span')
The draws below stay inside these ranges and needn't reach their ends.
Inputs may be any that keep to these rules, and one draw needn't show every extreme that they name: `pivot_inverse`: diagonal entries of each block are between 0.5 and 2; off-diagonal entries have magnitude at most 0.15. `lower_coupling`: diagonal entries of each block are between -1 and -0.8; off-diagonal entries have magnitude at most 0.025. `upper_coupling`: diagonal entries of each block are between -1 and -0.8; off-diagonal entries have magnitude at most 0.025.
All inputs are finite; a program needn't handle non-finite values.
Results may differ from the reference program's by a relative error of at most 0.0003.
Values sent between devices are 32-bit elements; how exact they have to be, the bound alone decides.
A program may use at most 192 MiB of HBM per device.

```python
import math
import jax
import jax.numpy as jnp
from jax import lax

NV = 5
NK = 4
NI = 1024
NJ = 1024


def identity_table():
    rows = lax.broadcasted_iota(jnp.int32, (NV, NV, 1, 1, 1), 0)
    cols = lax.broadcasted_iota(jnp.int32, (NV, NV, 1, 1, 1), 1)
    return (rows == cols).astype(jnp.float32)


def coupling_block(key, slowest):
    first, second, third = jax.random.split(key, 3)
    line_rate = jnp.exp(jax.random.uniform(first, (NV, 1, NK, 1, NJ), jnp.float32, math.log(slowest), math.log(0.12)))
    rough = jax.random.uniform(second, (NV, 1, NK, NI, NJ), jnp.float32, 0.5, 1.5)
    keep = 1.0 - jnp.minimum(line_rate * rough, 0.2)
    offdiag = 0.0249 * jax.random.uniform(third, (NV, NV, NK, NI, NJ), jnp.float32, -1.0, 1.0)
    table = identity_table()
    return (-(table * keep + (1.0 - table) * offdiag)).astype(jnp.bfloat16)


def draw_lower_coupling(key, part):
    key = jax.random.fold_in(key, 1)
    return coupling_block(key, 0.3 / NI)


def draw_upper_coupling(key, part):
    key = jax.random.fold_in(key, 2)
    return coupling_block(key, 0.3 / NI)


def draw_pivot_inverse(key, part):
    key = jax.random.fold_in(key, 3)
    first, second = jax.random.split(key)
    diagonal = jnp.exp(jax.random.uniform(first, (1, NV, NK, NI, NJ), jnp.float32, math.log(0.5), math.log(2.0)))
    offdiag = 0.149 * jax.random.uniform(second, (NV, NV, NK, NI, NJ), jnp.float32, -1.0, 1.0)
    table = identity_table()
    return (table * diagonal + (1.0 - table) * offdiag).astype(jnp.bfloat16)


def span_block(key):
    first, second = jax.random.split(key)
    line_rate = jnp.exp(jax.random.uniform(first, (NV, NK, NI, 1), jnp.float32, math.log(0.3 / NJ), math.log(0.12)))
    rough = jax.random.uniform(second, (NV, NK, NI, NJ), jnp.float32, 0.5, 1.5)
    return -(1.0 - jnp.minimum(line_rate * rough, 0.2))


def draw_span_lower(key, part):
    key = jax.random.fold_in(key, 4)
    return span_block(key)


def draw_span_upper(key, part):
    key = jax.random.fold_in(key, 5)
    return span_block(key)


def steps_of(key, extent, cuts, low, high):
    def one(dim, parts):
        draws = jax.random.uniform(jax.random.fold_in(jax.random.fold_in(key, 6), dim), (parts,), jnp.float32, low / len(cuts), high / len(cuts))
        return jnp.repeat(jnp.exp(draws), extent[dim] // parts).reshape((-1,) + (1,) * (len(extent) - dim - 1))

    gain = one(*cuts[0])
    for cut in cuts[1:]:
        gain = gain * one(*cut)
    return gain


def bell_draw(rng, dims, spread, reach, pieces=(), kind=jnp.bfloat16):
    entries = jax.random.normal(rng, dims, jnp.float32) * spread
    if len(pieces) > 0:
        entries = steps_of(rng, dims, pieces, -0.22, 0.18) * entries
    return jnp.clip(entries, min=-reach, max=reach).astype(kind)


def setup_inputs(seed: int = 0) -> dict:
    splits = jax.random.split(jax.random.key(seed), 11)
    return {
        "residual": bell_draw(splits[0], (NV, NK, NI, NJ), 1.0, 6.0, ((2, 32), (3, 8)), jnp.float32),
        "pivot_inverse": draw_pivot_inverse(jax.random.fold_in(splits[10], 71), 0),
        "lower_coupling": draw_lower_coupling(jax.random.fold_in(splits[10], 71), 0),
        "upper_coupling": draw_upper_coupling(jax.random.fold_in(splits[10], 71), 0),
        "span_pivot": jnp.clip(jnp.exp(math.log(2.0) - 1.3862944 * jax.random.uniform(splits[4], (NV, NK, NI, NJ), jnp.float32) ** steps_of(splits[4], (NV, NK, NI, NJ), ((2, 32), (3, 8)), -0.2, 0.2)), 0.5, 2.0),
        "span_lower": draw_span_lower(jax.random.fold_in(splits[10], 71), 0),
        "span_upper": draw_span_upper(jax.random.fold_in(splits[10], 71), 0),
        "normal_pivot": jnp.clip(jnp.exp(math.log(2.0) - 1.3862944 * jax.random.uniform(splits[7], (NV, NK, NI, NJ), jnp.float32) ** steps_of(splits[7], (NV, NK, NI, NJ), ((2, 32), (3, 8)), -0.2, 0.2)), 0.5, 2.0).astype(jnp.bfloat16),
        "normal_lower": jnp.clip(-0.8984375 + 0.69921875 * jax.random.uniform(splits[8], (NV, NK, NI, NJ), jnp.float32) ** steps_of(splits[8], (NV, NK, NI, NJ), ((2, 32), (3, 8)), -0.2, 0.2), -0.8984375, -0.19921875).astype(jnp.bfloat16),
        "normal_upper": jnp.clip(-0.84765625 + 0.59765625 * jax.random.uniform(splits[9], (NV, NK, NI, NJ), jnp.float32) ** steps_of(splits[9], (NV, NK, NI, NJ), ((2, 32), (3, 8)), -0.2, 0.2), -0.84765625, -0.25).astype(jnp.bfloat16),
    }


def product(matrix, other):
    total = matrix[:, 0:1] * other[0:1]
    for index in range(1, matrix.shape[1]):
        total = total + matrix[:, index:index + 1] * other[index:index + 1]
    return total


def normal_solve(values, pivots, lowers, uppers):
    pivots = pivots.astype(jnp.float32)
    lowers = lowers.astype(jnp.float32)
    uppers = uppers.astype(jnp.float32)
    planes = []
    carry = jnp.zeros_like(values[:, 0])
    for plane in range(values.shape[1]):
        carry = pivots[:, plane] * values[:, plane] - lowers[:, plane] * carry
        planes.append(carry)
    results = [None] * values.shape[1]
    carry = jnp.zeros_like(values[:, 0])
    for plane in reversed(range(values.shape[1])):
        carry = planes[plane] - uppers[:, plane] * carry
        results[plane] = carry
    return jnp.stack(results, axis=1)


def reference(residual, pivot_inverse, lower_coupling, upper_coupling, span_pivot, span_lower, span_upper, normal_pivot, normal_lower, normal_upper):
    def forward(carry, index):
        cells = lax.dynamic_index_in_dim(residual, index, 2, keepdims=False)[:, None]
        pivots = lax.dynamic_index_in_dim(pivot_inverse, index, 3, keepdims=False).astype(jnp.float32)
        lowers = lax.dynamic_index_in_dim(lower_coupling, index, 3, keepdims=False).astype(jnp.float32)
        result = product(pivots, cells) - product(lowers, carry)
        return result, result

    start = jnp.zeros((NV, 1, NK, NJ), jnp.float32)
    indices = jnp.arange(NI, dtype=jnp.int32)
    _, sweep = lax.scan(forward, start, indices)

    def backward(carry, pair):
        index, value = pair
        uppers = lax.dynamic_index_in_dim(upper_coupling, index, 3, keepdims=False).astype(jnp.float32)
        result = value - product(uppers, carry)
        return result, result

    _, chord = lax.scan(backward, start, (indices, sweep), reverse=True)
    chord = jnp.moveaxis(chord[:, :, 0], 0, 2)

    moved = [jnp.moveaxis(array, 3, 0) for array in (chord, span_pivot, span_lower, span_upper)]

    def span_forward(carry, cells):
        value, pivots, lowers = cells
        result = pivots * value - lowers * carry
        return result, result

    def span_backward(carry, cells):
        value, uppers = cells
        result = value - uppers * carry
        return result, result

    zeros = jnp.zeros((NV, NK, NI), jnp.float32)
    _, swept = lax.scan(span_forward, zeros, (moved[0], moved[1], moved[2]))
    _, spanned = lax.scan(span_backward, zeros, (swept, moved[3]), reverse=True)
    spanned = jnp.moveaxis(spanned, 0, 3)
    return normal_solve(spanned, normal_pivot, normal_lower, normal_upper)
```

```python
import functools

import jax
import jax.numpy as jnp
from jax import lax
from jax.experimental import pallas as pl
from jax.experimental.pallas import tpu as pltpu
from jax.sharding import PartitionSpec as P

F32 = jnp.float32
MESH = pl.DeviceIdType.MESH

NV = 5
NK = 4
CHORD = 32
SPAN = 8
CELLS = 32
LANES = 128
HALF = 16
GROUPS = 11
MAT, VEC, OUT, INN, SRC = 0, 25, 30, 55, 80


def dot(lhs, rhs):
    terms = [a * b for a, b in zip(lhs, rhs)]
    while len(terms) > 1:
        terms = [terms[i] + terms[i + 1] if i + 1 < len(terms) else terms[i] for i in range(0, len(terms), 2)]
    return terms[0]


def column(matrix, index):
    return [row[index] for row in matrix]


def matmul(lhs, rhs):
    cols = [column(rhs, j) for j in range(len(rhs[0]))]
    return [[dot(row, col) for col in cols] for row in lhs]


def matvec(lhs, vec):
    return [dot(row, vec) for row in lhs]


def block_transpose(tile, sub, blk):
    for d in (4, 2, 1):
        s_bit = (sub & d) != 0
        b_bit = (blk & d) != 0
        if d == 4:
            other = pltpu.roll(pltpu.roll(tile, 4, 0), 64, 1)
        else:
            up = pltpu.roll(pltpu.roll(tile, 8 - d, 0), 16 * d, 1)
            down = pltpu.roll(pltpu.roll(tile, d, 0), 128 - 16 * d, 1)
            other = jnp.where(s_bit, down, up)
        tile = jnp.where(s_bit == b_bit, tile, other)
    return tile


def kernel(
    res_h, piv_h, low_h, upp_h, sp_h, sl_h, su_h, np_h, nl_h, nu_h,
    out_ref,
    res, piv, low, upp, spn, sln, sun, npn, nln, nun,
    pivf, lowf, uppf, source, state, comb, send1, recv1, expand, entry, total,
    send2, recv2, unsh, carry, ysweep, wnat,
    wt, pt, lt, ut, gain, pre, alp, bet, cc, aa,
    gsend, grecv, hsend, hrecv, sentry,
    load_sem, sems,
):
    me_c = lax.axis_index("chord")
    me_s = lax.axis_index("span")

    loads = []
    for n, (src, dst) in enumerate(
        [(res_h, res), (piv_h, piv), (low_h, low), (upp_h, upp), (sp_h, spn), (sl_h, sln), (su_h, sun),
         (np_h, npn), (nl_h, nln), (nu_h, nun)]
    ):
        copy = pltpu.make_async_copy(src, dst, load_sem.at[n])
        copy.start()
        loads.append(copy)

    barrier = pltpu.get_barrier_semaphore()

    def greet_chord(o, _):
        pl.semaphore_signal(barrier, inc=1, device_id={"chord": lax.rem(me_c + o, CHORD)}, device_id_type=MESH)
        return 0

    def greet_span(o, _):
        pl.semaphore_signal(barrier, inc=1, device_id={"span": lax.rem(me_s + o, SPAN)}, device_id_type=MESH)
        return 0

    lax.fori_loop(1, CHORD, greet_chord, 0)
    lax.fori_loop(1, SPAN, greet_span, 0)

    sub = lax.broadcasted_iota(jnp.int32, (8, LANES), 0)
    lane = lax.broadcasted_iota(jnp.int32, (8, LANES), 1)
    blk = lane // 16

    def widen(src, dst):
        def body(n, _):
            rows = pl.ds(pl.multiple_of(n * 128, 128), 128)
            dst[rows] = src[rows].astype(F32)
            return 0

        lax.fori_loop(0, NV * NV, body, 0)

    loads[1].wait()
    widen(piv, pivf)
    loads[2].wait()
    widen(low, lowf)
    loads[3].wait()
    widen(upp, uppf)
    loads[0].wait()

    zero = jnp.zeros((8, LANES), F32)
    one = jnp.ones((8, LANES), F32)

    def tile_of(value):
        return pl.ds(8 * value, 8)

    for r in range(NV):
        for c in range(NV):
            state[tile_of(MAT + 5 * r + c)] = one if r == c else zero
            state[tile_of(OUT + 5 * r + c)] = one if r == c else zero
            state[tile_of(INN + 5 * r + c)] = zero
        state[tile_of(VEC + r)] = zero
        state[tile_of(SRC + r)] = zero

    def block(ref, index, step):
        return ref[pl.ds(index * 128 + step, 8, stride=HALF)]

    def blocks(ref, step):
        return [[block(ref, 5 * r + c, step) for c in range(NV)] for r in range(NV)]

    def map_step(pair, _):
        for odd in range(2):
            step = 2 * pair + odd
            cells = [block(res, c, step) for c in range(NV)]
            src = [dot([block(pivf, 5 * r + c, step) for c in range(NV)], cells) for r in range(NV)]
            for r in range(NV):
                source[pl.ds(pl.multiple_of((step * NV + r) * 8, 8), 8)] = src[r]
            lows = blocks(lowf, step)
            cols = []
            for c in range(NV):
                new = matvec(lows, [state[tile_of(MAT + 5 * r + c)] for r in range(NV)])
                for r in range(NV):
                    state[tile_of(MAT + 5 * r + c)] = new[r]
                cols.append(new)
            new = matvec(lows, [state[tile_of(VEC + r)] for r in range(NV)])
            new = [n + s if odd else n - s for n, s in zip(new, src)]
            for r in range(NV):
                state[tile_of(VEC + r)] = new[r]
            cols.append(new)
            upps = blocks(uppf, step)
            for r in range(NV):
                row = [state[tile_of(OUT + 5 * r + c)] for c in range(NV)]
                for c in range(NV):
                    at = tile_of(INN + 5 * r + c)
                    state[at] = state[at] + dot(row, cols[c])
                at = tile_of(SRC + r)
                state[at] = state[at] + dot(row, cols[NV])
                for c in range(NV):
                    state[tile_of(OUT + 5 * r + c)] = dot(row, column(upps, c))
        return 0

    lax.fori_loop(0, HALF // 2, map_step, 0)

    def half(value, which):
        return state[pl.ds(8 * value + which, NK, stride=2)]

    def half_matrix(base, which):
        return [[half(base + 5 * r + c, which) for c in range(NV)] for r in range(NV)]

    def half_vector(base, which):
        return [half(base + r, which) for r in range(NV)]

    def put(value, data):
        comb[pl.ds(NK * value, NK)] = data

    mat0 = half_matrix(MAT, 0)
    vec0 = half_vector(VEC, 0)
    mat1 = half_matrix(MAT, 1)
    mats = matmul(mat1, mat0)
    vecs = matvec(mat1, vec0)
    for r in range(NV):
        for c in range(NV):
            put(MAT + 5 * r + c, mats[r][c])
        put(VEC + r, vecs[r] + half(VEC + r, 1))
    inn1 = half_matrix(INN, 1)
    part = matmul(inn1, mat0)
    tail = [t + half(SRC + r, 1) for r, t in enumerate(matvec(inn1, vec0))]
    out0 = half_matrix(OUT, 0)
    outs = matmul(out0, half_matrix(OUT, 1))
    inns = matmul(out0, part)
    srcs = matvec(out0, tail)
    for r in range(NV):
        for c in range(NV):
            put(OUT + 5 * r + c, outs[r][c])
            put(INN + 5 * r + c, inns[r][c] + half(INN + 5 * r + c, 0))
        put(SRC + r, srcs[r] + half(SRC + r, 0))
    for value in range(85, 88):
        put(value, jnp.zeros((NK, LANES), F32))

    def shuffle(k, _):
        for g in range(GROUPS):
            tile = comb[pl.ds(NK * 8 * g + k, 8, stride=NK)]
            send1[pl.ds(8 * GROUPS * k + g, 8, stride=GROUPS), 0] = block_transpose(tile, sub, blk)
        return 0

    lax.fori_loop(0, NK, shuffle, 0)

    pl.semaphore_wait(barrier, CHORD - 1 + SPAN - 1)

    def exchange(send, recv, rows, count, me, axis, at):
        def start(o, _):
            to = lax.rem(me + o, count)
            pltpu.make_async_remote_copy(
                src_ref=send.at[pl.ds(to * rows, rows)],
                dst_ref=recv.at[pl.ds(me * rows, rows)],
                send_sem=sems.at[2 * at],
                recv_sem=sems.at[2 * at + 1],
                device_id={axis: to},
                device_id_type=MESH,
            ).start()
            return 0

        lax.fori_loop(1, count, start, 0)
        recv[pl.ds(me * rows, rows)] = send[pl.ds(me * rows, rows)]

    def spread(send, recv, rows, at):
        def start(o, _):
            pltpu.make_async_remote_copy(
                src_ref=send,
                dst_ref=recv.at[pl.ds(me_s * rows, rows)],
                send_sem=sems.at[2 * at],
                recv_sem=sems.at[2 * at + 1],
                device_id={"span": lax.rem(me_s + o, SPAN)},
                device_id_type=MESH,
            ).start()
            return 0

        lax.fori_loop(1, SPAN, start, 0)
        recv[pl.ds(me_s * rows, rows)] = send[...]

    def settle(ref, rows, sem):
        whole = ref.at[pl.ds(0, rows)]
        pltpu.make_async_copy(whole, whole, sems.at[sem]).wait()

    exchange(send1, recv1, GROUPS, CHORD, me_c, "chord", 0)

    for n, (src, dst) in enumerate([(spn, pt), (sln, lt), (sun, ut)]):
        loads[4 + n].wait()
        for v in range(NV):
            dst[pl.ds(v, LANES, stride=8)] = src[pl.ds(128 * v, 128)].T

    def at_j(j):
        return pl.ds(pl.multiple_of(8 * j, 8), NV)

    ones5 = jnp.ones((NV, LANES), F32)
    zeros5 = jnp.zeros((NV, LANES), F32)

    def gains_ahead(j, held):
        g, p = held
        g = -(lt[at_j(j)] * g)
        gain[at_j(j)] = g
        pre[at_j(j)] = p
        return (g, -(ut[at_j(j)] * p))

    g_end, _ = lax.fori_loop(0, LANES, gains_ahead, (ones5, ones5), unroll=8)

    def gains_back(n, held):
        suf, b, c, a, low_next = held
        j = LANES - 1 - n
        l, u, p = lt[at_j(j)], ut[at_j(j)], pt[at_j(j)]
        alp[at_j(j)] = suf * p
        b = pre[at_j(j)] - low_next * b
        bet[at_j(j)] = b * p
        c = -(u * c)
        cc[at_j(j)] = c
        a = gain[at_j(j)] - u * a
        aa[at_j(j)] = a
        return (-(l * suf), b, c, a, l)

    _, _, c_top, a_top, _ = lax.fori_loop(
        0, LANES, gains_back, (ones5, zeros5, ones5, zeros5, zeros5), unroll=8
    )
    gsend[pl.ds(0, NV), 0] = g_end
    gsend[pl.ds(NV, NV), 0] = a_top
    gsend[pl.ds(2 * NV, NV), 0] = c_top
    spread(gsend, grecv, 3 * NV, 2)

    settle(recv1, (CHORD - 1) * GROUPS, 1)

    def unpack(q, _):
        for g in range(GROUPS):
            tile = recv1[pl.ds(8 * GROUPS * q + g, 8, stride=GROUPS), 0]
            for s in range(8):
                value = 8 * g + s
                if value < 85:
                    moved = tile if s == 0 else pltpu.roll(tile, LANES - 16 * s, 1)
                    expand[pl.ds(pl.multiple_of(CHORD * value + 8 * q, 8), 8)] = moved
        return 0

    lax.fori_loop(0, CHORD // 8, unpack, 0)

    def row(value, at):
        return expand[pl.ds(CHORD * value + at, 1)]

    def relay_ahead(at, held):
        new = []
        for c in range(NV):
            entry[pl.ds(CHORD * c + at, 1)] = held[c]
        for r in range(NV):
            new.append(dot([row(MAT + 5 * r + c, at) for c in range(NV)], held) + row(VEC + r, at))
        return tuple(new)

    nothing = tuple(jnp.zeros((1, LANES), F32) for _ in range(NV))
    lax.fori_loop(0, CHORD, relay_ahead, nothing, unroll=4)

    for q in range(CHORD // 8):
        vec = [entry[pl.ds(CHORD * c + 8 * q, 8)] for c in range(NV)]
        for r in range(NV):
            mats_r = [expand[pl.ds(CHORD * (INN + 5 * r + c) + 8 * q, 8)] for c in range(NV)]
            total[pl.ds(CHORD * r + 8 * q, 8)] = -(dot(mats_r, vec) + expand[pl.ds(CHORD * (SRC + r) + 8 * q, 8)])

    def relay_back(n, held):
        at = CHORD - 1 - n
        new = []
        for c in range(NV):
            entry[pl.ds(CHORD * (NV + c) + at, 1)] = held[c]
        for r in range(NV):
            new.append(
                dot([row(OUT + 5 * r + c, at) for c in range(NV)], held) + total[pl.ds(CHORD * r + at, 1)]
            )
        return tuple(new)

    lax.fori_loop(0, CHORD, relay_back, nothing, unroll=4)

    for q in range(CHORD // 8):
        for kind in range(2):
            tile = zero
            for s in range(NV):
                part_s = entry[pl.ds(CHORD * (NV * kind + s) + 8 * q, 8)]
                if s > 0:
                    part_s = pltpu.roll(part_s, 16 * s, 1)
                tile = jnp.where(blk == s, part_s, tile)
            send2[pl.ds(16 * q + kind, 8, stride=2), 0] = tile

    exchange(send2, recv2, 2, CHORD, me_c, "chord", 1)
    settle(recv2, (CHORD - 1) * 2, 3)

    for kind in range(2):
        for k in range(NK):
            tile = recv2[pl.ds(16 * k + kind, 8, stride=2), 0]
            unsh[pl.ds(8 * (NK * kind + k), 8)] = block_transpose(tile, sub, blk)
    a0 = [unsh[pl.ds(v, NK, stride=8)] for v in range(NV)]
    c1 = [unsh[pl.ds(8 * NK + v, NK, stride=8)] for v in range(NV)]
    a1 = [m + half(VEC + r, 0) for r, m in enumerate(matvec(half_matrix(MAT, 0), a0))]
    back = matvec(half_matrix(OUT, 1), c1)
    fore = matvec(half_matrix(INN, 1), a1)
    c0 = [back[r] - (fore[r] + half(SRC + r, 1)) for r in range(NV)]
    for v in range(NV):
        carry[pl.ds(8 * v, NK, stride=2)] = a0[v]
        carry[pl.ds(8 * v + 1, NK, stride=2)] = a1[v]
        carry[pl.ds(8 * (NV + v), NK, stride=2)] = c0[v]
        carry[pl.ds(8 * (NV + v) + 1, NK, stride=2)] = c1[v]

    def sweep_ahead(step, held):
        new = []
        for r in range(NV):
            at = pl.ds(pl.multiple_of((step * NV + r) * 8, 8), 8)
            val = source[at] - dot([block(lowf, 5 * r + c, step) for c in range(NV)], held)
            ysweep[at] = val
            new.append(val)
        return tuple(new)

    lax.fori_loop(0, HALF, sweep_ahead, tuple(carry[tile_of(v)] for v in range(NV)), unroll=4)

    def sweep_back(n, held):
        step = HALF - 1 - n
        new = []
        for r in range(NV):
            at = pl.ds(pl.multiple_of((step * NV + r) * 8, 8), 8)
            val = ysweep[at] - dot([block(uppf, 5 * r + c, step) for c in range(NV)], held)
            wnat[pl.ds(128 * r + step, 8, stride=HALF)] = val
            new.append(val)
        return tuple(new)

    lax.fori_loop(0, HALF, sweep_back, tuple(carry[tile_of(NV + v)] for v in range(NV)), unroll=4)

    for v in range(NV):
        wt[pl.ds(v, LANES, stride=8)] = wnat[pl.ds(128 * v, 128)].T

    def ends(j, held):
        h, w0 = held
        w = wt[at_j(j)]
        return (h + alp[at_j(j)] * w, w0 + bet[at_j(j)] * w)

    h, w0 = lax.fori_loop(0, LANES, ends, (zeros5, zeros5), unroll=8)
    hsend[pl.ds(0, NV), 0] = h
    hsend[pl.ds(NV, NV), 0] = w0
    spread(hsend, hrecv, 2 * NV, 3)

    def span_ahead(j, z):
        z = pt[at_j(j)] * wt[at_j(j)] - lt[at_j(j)] * z
        wt[at_j(j)] = z
        return z

    lax.fori_loop(0, LANES, span_ahead, zeros5, unroll=8)

    def span_back(n, z):
        j = LANES - 1 - n
        z = wt[at_j(j)] - ut[at_j(j)] * z
        wt[at_j(j)] = z
        return z

    lax.fori_loop(0, LANES, span_back, zeros5, unroll=8)

    settle(grecv, (SPAN - 1) * 3 * NV, 5)
    settle(hrecv, (SPAN - 1) * 2 * NV, 7)
    a = zeros5
    sent = []
    for d in range(SPAN):
        sentry[pl.ds(8 * d, NV)] = a
        sent.append(a)
        a = hrecv[pl.ds(2 * NV * d, NV), 0] + grecv[pl.ds(3 * NV * d, NV), 0] * a
    c = zeros5
    for d in reversed(range(SPAN)):
        sentry[pl.ds(8 * (SPAN + d), NV)] = c
        c = (
            hrecv[pl.ds(2 * NV * d + NV, NV), 0]
            + grecv[pl.ds(3 * NV * d + NV, NV), 0] * sent[d]
            + grecv[pl.ds(3 * NV * d + 2 * NV, NV), 0] * c
        )
    a_in = sentry[pl.ds(pl.multiple_of(8 * me_s, 8), NV)]
    c_in = sentry[pl.ds(pl.multiple_of(8 * (SPAN + me_s), 8), NV)]

    def close(j, _):
        wt[at_j(j)] = wt[at_j(j)] + aa[at_j(j)] * a_in + cc[at_j(j)] * c_in
        return 0

    lax.fori_loop(0, LANES, close, 0, unroll=8)

    for n in range(7, 10):
        loads[n].wait()
    for v in range(NV):
        x = wt[pl.ds(v, LANES, stride=8)].T
        held = None
        planes = []
        for k in range(NK):
            at = pl.ds(128 * v + 32 * k, 32)
            now = npn[at].astype(F32) * x[32 * k : 32 * k + 32]
            held = now if held is None else now - nln[at].astype(F32) * held
            planes.append(held)
        held = None
        for k in reversed(range(NK)):
            at = pl.ds(128 * v + 32 * k, 32)
            held = planes[k] if held is None else planes[k] - nun[at].astype(F32) * held
            out_ref[at] = held

    settle(send1, (CHORD - 1) * GROUPS, 0)
    settle(send2, (CHORD - 1) * 2, 2)
    settle(grecv, (SPAN - 1) * 3 * NV, 4)
    settle(hrecv, (SPAN - 1) * 2 * NV, 6)


def on_device(*args):
    flat = [a.reshape(-1, LANES) for a in args]
    f32 = lambda *shape: pltpu.VMEM(shape, F32)
    b16 = lambda *shape: pltpu.VMEM(shape, jnp.bfloat16)
    wide, narrow = NV * NV * 128, NV * 128
    scratch = [
        f32(narrow, LANES), b16(wide, LANES), b16(wide, LANES), b16(wide, LANES),
        f32(narrow, LANES), f32(narrow, LANES), f32(narrow, LANES),
        b16(narrow, LANES), b16(narrow, LANES), b16(narrow, LANES),
        f32(wide, LANES), f32(wide, LANES), f32(wide, LANES),
        f32(HALF * NV * 8, LANES),
        f32(88 * 8, LANES),
        f32(88 * NK, LANES),
        f32(CHORD * GROUPS, 1, LANES), f32(CHORD * GROUPS, 1, LANES),
        f32(88 * CHORD, LANES),
        f32(2 * NV * CHORD, LANES), f32(NV * CHORD, LANES),
        f32(2 * CHORD, 1, LANES), f32(2 * CHORD, 1, LANES),
        f32(64, LANES), f32(80, LANES),
        f32(HALF * NV * 8, LANES), f32(narrow, LANES),
    ]
    scratch += [f32(8 * LANES, LANES) for _ in range(10)]
    scratch += [
        f32(3 * NV, 1, LANES), f32(SPAN * 3 * NV, 1, LANES),
        f32(2 * NV, 1, LANES), f32(SPAN * 2 * NV, 1, LANES),
        f32(2 * SPAN * 8, LANES),
        pltpu.SemaphoreType.DMA((10,)),
        pltpu.SemaphoreType.DMA((8,)),
    ]
    out = pl.pallas_call(
        kernel,
        out_shape=jax.ShapeDtypeStruct((narrow, LANES), F32),
        in_specs=[pl.BlockSpec(memory_space=pl.ANY)] * 10,
        out_specs=pl.BlockSpec(memory_space=pltpu.VMEM),
        scratch_shapes=scratch,
        compiler_params=pltpu.CompilerParams(
            collective_id=0, has_side_effects=True, vmem_limit_bytes=40 * 1024 * 1024
        ),
    )(*flat)
    return out.reshape(NV, NK, CELLS, LANES)


def solution(mesh):
    grid = P(None, None, "chord", "span")
    deep = P(None, None, None, "chord", "span")
    return jax.shard_map(
        on_device,
        mesh=mesh,
        in_specs=(grid, deep, deep, deep, grid, grid, grid, grid, grid, grid),
        out_specs=grid,
        check_vma=False,
    )
```

```python
import functools

import jax
import jax.numpy as jnp
from jax import lax
from jax.experimental import pallas as pl
from jax.experimental.pallas import tpu as pltpu
from jax.sharding import PartitionSpec as P

F32 = jnp.float32
MESH = pl.DeviceIdType.MESH

NV = 5
NK = 4
CHORD = 32
SPAN = 8
CELLS = 32
LANES = 128
HALF = 16
GROUPS = 11
MAT, VEC, OUT, INN, SRC = 0, 25, 30, 55, 80
ZS, XS = 8, 4


def ring(step, size):
    return min(step, size - step)


CHORD_PEERS = sorted(
    [(dz, dx) for dz in range(ZS) for dx in range(XS) if dz or dx], key=lambda p: -ring(p[0], ZS) - ring(p[1], XS)
)
SPAN_PEERS = (4, 5, 3, 2, 6, 7, 1)


def dot(lhs, rhs):
    terms = [a * b for a, b in zip(lhs, rhs)]
    while len(terms) > 1:
        terms = [terms[i] + terms[i + 1] if i + 1 < len(terms) else terms[i] for i in range(0, len(terms), 2)]
    return terms[0]


def affine(lhs, rhs, extra):
    a, b, c, d, e = [x * y for x, y in zip(lhs, rhs)]
    return ((a + b) + (c + d)) + (e + extra)


def residue(extra, lhs, rhs):
    a, b, c, d, e = [x * y for x, y in zip(lhs, rhs)]
    return (extra - e) - ((a + b) + (c + d))


def column(matrix, index):
    return [row[index] for row in matrix]


def matmul(lhs, rhs):
    cols = [column(rhs, j) for j in range(len(rhs[0]))]
    return [[dot(row, col) for col in cols] for row in lhs]


def matvec(lhs, vec):
    return [dot(row, vec) for row in lhs]


def block_transpose(tile, sub, blk):
    for d in (4, 2, 1):
        s_bit = (sub & d) != 0
        b_bit = (blk & d) != 0
        if d == 4:
            other = pltpu.roll(pltpu.roll(tile, 4, 0), 64, 1)
        else:
            up = pltpu.roll(pltpu.roll(tile, 8 - d, 0), 16 * d, 1)
            down = pltpu.roll(pltpu.roll(tile, d, 0), 128 - 16 * d, 1)
            other = jnp.where(s_bit, down, up)
        tile = jnp.where(s_bit == b_bit, tile, other)
    return tile


def kernel(
    res_h, piv_h, low_h, upp_h, sp_h, sl_h, su_h, np_h, nl_h, nu_h,
    out_ref,
    res, piv, low, upp, spn, sln, sun, npn, nln, nun,
    pivf, lowf, uppf, source, state, comb, send1, recv1, expand, entry, total,
    send2, recv2, unsh, carry, ysweep, wnat,
    wt, pt, lt, ut, gain, pre, alp, bet, cc, aa,
    gsend, grecv, hsend, hrecv, sentry,
    lows_by, upps_by, wvar, alp_v, bet_v,
    load_sem, sems,
):
    me_c = lax.axis_index("chord")
    me_s = lax.axis_index("span")

    z, x = me_c // XS, lax.rem(me_c, XS)

    def chord_peer(peer):
        return lax.rem(z + peer[0], ZS) * XS + lax.rem(x + peer[1], XS)

    barrier = pltpu.get_barrier_semaphore()
    for peer in CHORD_PEERS:
        pl.semaphore_signal(barrier, inc=1, device_id={"chord": chord_peer(peer)}, device_id_type=MESH)
    for o in SPAN_PEERS:
        pl.semaphore_signal(barrier, inc=1, device_id={"span": lax.rem(me_s + o, SPAN)}, device_id_type=MESH)

    loads = {}
    for n, src, dst in [
        (1, piv_h, piv), (0, res_h, res), (2, low_h, low), (3, upp_h, upp), (4, sp_h, spn), (5, sl_h, sln),
        (6, su_h, sun), (7, np_h, npn), (8, nl_h, nln), (9, nu_h, nun),
    ]:
        copy = pltpu.make_async_copy(src, dst, load_sem.at[n])
        copy.start()
        loads[n] = copy

    sub = lax.broadcasted_iota(jnp.int32, (8, LANES), 0)
    lane = lax.broadcasted_iota(jnp.int32, (8, LANES), 1)
    blk = lane // 16

    def widen(src, dst):
        def body(n, _):
            rows = pl.ds(pl.multiple_of(n * 128, 128), 128)
            dst[rows] = src[rows].astype(F32)
            return 0

        lax.fori_loop(0, NV * NV, body, 0)

    loads[1].wait()
    widen(piv, pivf)
    loads[2].wait()
    widen(low, lowf)
    loads[3].wait()
    widen(upp, uppf)
    loads[0].wait()

    zero = jnp.zeros((8, LANES), F32)
    one = jnp.ones((8, LANES), F32)

    def tile_of(value):
        return pl.ds(8 * value, 8)

    for r in range(NV):
        for c in range(NV):
            state[tile_of(MAT + 5 * r + c)] = one if r == c else zero
            state[tile_of(OUT + 5 * r + c)] = one if r == c else zero
            state[tile_of(INN + 5 * r + c)] = zero
        state[tile_of(VEC + r)] = zero
        state[tile_of(SRC + r)] = zero

    def block(ref, index, step):
        return ref[pl.ds(index * 128 + step, 8, stride=HALF)]

    def blocks(ref, step):
        return [[block(ref, 5 * r + c, step) for c in range(NV)] for r in range(NV)]

    def map_step(pair, _):
        for odd in range(2):
            step = 2 * pair + odd
            cells = [block(res, c, step) for c in range(NV)]
            src = [dot([block(pivf, 5 * r + c, step) for c in range(NV)], cells) for r in range(NV)]
            for r in range(NV):
                source[pl.ds(pl.multiple_of((step * NV + r) * 8, 8), 8)] = src[r]
            lows = blocks(lowf, step)
            cols = []
            for c in range(NV):
                new = matvec(lows, [state[tile_of(MAT + 5 * r + c)] for r in range(NV)])
                for r in range(NV):
                    state[tile_of(MAT + 5 * r + c)] = new[r]
                cols.append(new)
            new = matvec(lows, [state[tile_of(VEC + r)] for r in range(NV)])
            new = [n + s if odd else n - s for n, s in zip(new, src)]
            for r in range(NV):
                state[tile_of(VEC + r)] = new[r]
            cols.append(new)
            upps = blocks(uppf, step)
            for r in range(NV):
                row = [state[tile_of(OUT + 5 * r + c)] for c in range(NV)]
                for c in range(NV):
                    at = tile_of(INN + 5 * r + c)
                    state[at] = state[at] + dot(row, cols[c])
                at = tile_of(SRC + r)
                state[at] = state[at] + dot(row, cols[NV])
                for c in range(NV):
                    state[tile_of(OUT + 5 * r + c)] = dot(row, column(upps, c))
        return 0

    lax.fori_loop(0, HALF // 2, map_step, 0)

    def half(value, which):
        return state[pl.ds(8 * value + which, NK, stride=2)]

    def half_matrix(base, which):
        return [[half(base + 5 * r + c, which) for c in range(NV)] for r in range(NV)]

    def half_vector(base, which):
        return [half(base + r, which) for r in range(NV)]

    def put(value, data):
        comb[pl.ds(NK * value, NK)] = data

    mat0 = half_matrix(MAT, 0)
    vec0 = half_vector(VEC, 0)
    mat1 = half_matrix(MAT, 1)
    mats = matmul(mat1, mat0)
    vecs = matvec(mat1, vec0)
    for r in range(NV):
        for c in range(NV):
            put(MAT + 5 * r + c, mats[r][c])
        put(VEC + r, vecs[r] + half(VEC + r, 1))
    inn1 = half_matrix(INN, 1)
    part = matmul(inn1, mat0)
    tail = [t + half(SRC + r, 1) for r, t in enumerate(matvec(inn1, vec0))]
    out0 = half_matrix(OUT, 0)
    outs = matmul(out0, half_matrix(OUT, 1))
    inns = matmul(out0, part)
    srcs = matvec(out0, tail)
    for r in range(NV):
        for c in range(NV):
            put(OUT + 5 * r + c, outs[r][c])
            put(INN + 5 * r + c, inns[r][c] + half(INN + 5 * r + c, 0))
        put(SRC + r, srcs[r] + half(SRC + r, 0))
    for value in range(85, 88):
        put(value, jnp.zeros((NK, LANES), F32))

    def shuffle(k, _):
        for g in range(GROUPS):
            tile = comb[pl.ds(NK * 8 * g + k, 8, stride=NK)]
            send1[pl.ds(8 * GROUPS * k + g, 8, stride=GROUPS), 0] = block_transpose(tile, sub, blk)
        return 0

    lax.fori_loop(0, NK, shuffle, 0)

    pl.semaphore_wait(barrier, CHORD - 1 + SPAN - 1)

    def exchange(send, recv, rows, at):
        for peer in CHORD_PEERS:
            to = chord_peer(peer)
            pltpu.make_async_remote_copy(
                src_ref=send.at[pl.ds(to * rows, rows)],
                dst_ref=recv.at[pl.ds(me_c * rows, rows)],
                send_sem=sems.at[2 * at],
                recv_sem=sems.at[2 * at + 1],
                device_id={"chord": to},
                device_id_type=MESH,
            ).start()
        recv[pl.ds(me_c * rows, rows)] = send[pl.ds(me_c * rows, rows)]

    def spread(send, recv, rows, at):
        for o in SPAN_PEERS:
            pltpu.make_async_remote_copy(
                src_ref=send,
                dst_ref=recv.at[pl.ds(me_s * rows, rows)],
                send_sem=sems.at[2 * at],
                recv_sem=sems.at[2 * at + 1],
                device_id={"span": lax.rem(me_s + o, SPAN)},
                device_id_type=MESH,
            ).start()
        recv[pl.ds(me_s * rows, rows)] = send[...]

    def settle(ref, rows, sem):
        whole = ref.at[pl.ds(0, rows)]
        pltpu.make_async_copy(whole, whole, sems.at[sem]).wait()

    exchange(send1, recv1, GROUPS, 0)

    for n, (src, dst) in enumerate([(spn, pt), (sln, lt), (sun, ut)]):
        loads[4 + n].wait()
        for v in range(NV):
            dst[pl.ds(v, LANES, stride=8)] = src[pl.ds(128 * v, 128)].T

    def at_j(j):
        return pl.ds(pl.multiple_of(8 * j, 8), NV)

    ones5 = jnp.ones((NV, LANES), F32)
    zeros5 = jnp.zeros((NV, LANES), F32)

    def gains_ahead(j, held):
        g, p = held
        g = -(lt[at_j(j)] * g)
        gain[at_j(j)] = g
        pre[at_j(j)] = p
        return (g, -(ut[at_j(j)] * p))

    g_end, _ = lax.fori_loop(0, LANES, gains_ahead, (ones5, ones5), unroll=8)

    def gains_back(n, held):
        suf, b, c, a, low_next = held
        j = LANES - 1 - n
        l, u, p = lt[at_j(j)], ut[at_j(j)], pt[at_j(j)]
        alp[at_j(j)] = suf * p
        b = pre[at_j(j)] - low_next * b
        bet[at_j(j)] = b * p
        c = -(u * c)
        cc[at_j(j)] = c
        a = gain[at_j(j)] - u * a
        aa[at_j(j)] = a
        return (-(l * suf), b, c, a, l)

    _, _, c_top, a_top, _ = lax.fori_loop(
        0, LANES, gains_back, (ones5, zeros5, ones5, zeros5, zeros5), unroll=8
    )
    gsend[pl.ds(0, NV), 0] = g_end
    gsend[pl.ds(NV, NV), 0] = a_top
    gsend[pl.ds(2 * NV, NV), 0] = c_top
    spread(gsend, grecv, 3 * NV, 2)
    for v in range(NV):
        alp_v[pl.ds(128 * v, 128)] = alp[pl.ds(v, LANES, stride=8)]
        bet_v[pl.ds(128 * v, 128)] = bet[pl.ds(v, LANES, stride=8)]

    settle(recv1, (CHORD - 1) * GROUPS, 1)

    def unpack(q, _):
        for g in range(GROUPS):
            tile = recv1[pl.ds(8 * GROUPS * q + g, 8, stride=GROUPS), 0]
            for s in range(8):
                value = 8 * g + s
                if value < 85:
                    moved = tile if s == 0 else pltpu.roll(tile, LANES - 16 * s, 1)
                    expand[pl.ds(pl.multiple_of(CHORD * value + 8 * q, 8), 8)] = moved
        return 0

    lax.fori_loop(0, CHORD // 8, unpack, 0)

    def row(value, at):
        return expand[pl.ds(CHORD * value + at, 1)]

    def relay_ahead(at, held):
        new = []
        for c in range(NV):
            entry[pl.ds(CHORD * c + at, 1)] = held[c]
        for r in range(NV):
            new.append(affine([row(MAT + 5 * r + c, at) for c in range(NV)], held, row(VEC + r, at)))
        return tuple(new)

    nothing = tuple(jnp.zeros((1, LANES), F32) for _ in range(NV))
    lax.fori_loop(0, CHORD, relay_ahead, nothing, unroll=4)

    for q in range(CHORD // 8):
        vec = [entry[pl.ds(CHORD * c + 8 * q, 8)] for c in range(NV)]
        for r in range(NV):
            mats_r = [expand[pl.ds(CHORD * (INN + 5 * r + c) + 8 * q, 8)] for c in range(NV)]
            total[pl.ds(CHORD * r + 8 * q, 8)] = -(dot(mats_r, vec) + expand[pl.ds(CHORD * (SRC + r) + 8 * q, 8)])

    def relay_back(n, held):
        at = CHORD - 1 - n
        new = []
        for c in range(NV):
            entry[pl.ds(CHORD * (NV + c) + at, 1)] = held[c]
        for r in range(NV):
            new.append(
                affine([row(OUT + 5 * r + c, at) for c in range(NV)], held, total[pl.ds(CHORD * r + at, 1)])
            )
        return tuple(new)

    lax.fori_loop(0, CHORD, relay_back, nothing, unroll=4)

    for q in range(CHORD // 8):
        for kind in range(2):
            tile = zero
            for s in range(NV):
                part_s = entry[pl.ds(CHORD * (NV * kind + s) + 8 * q, 8)]
                if s > 0:
                    part_s = pltpu.roll(part_s, 16 * s, 1)
                tile = jnp.where(blk == s, part_s, tile)
            send2[pl.ds(16 * q + kind, 8, stride=2), 0] = tile

    exchange(send2, recv2, 2, 1)

    def gather_steps(step, _):
        for index in range(NV * NV):
            at = pl.ds(pl.multiple_of((step * NV * NV + index) * 8, 8), 8)
            lows_by[at] = block(lowf, index, step)
            upps_by[at] = block(uppf, index, step)
        return 0

    lax.fori_loop(0, HALF, gather_steps, 0)
    settle(recv2, (CHORD - 1) * 2, 3)

    for kind in range(2):
        for k in range(NK):
            tile = recv2[pl.ds(16 * k + kind, 8, stride=2), 0]
            unsh[pl.ds(8 * (NK * kind + k), 8)] = block_transpose(tile, sub, blk)
    a0 = [unsh[pl.ds(v, NK, stride=8)] for v in range(NV)]
    c1 = [unsh[pl.ds(8 * NK + v, NK, stride=8)] for v in range(NV)]
    a1 = [m + half(VEC + r, 0) for r, m in enumerate(matvec(half_matrix(MAT, 0), a0))]
    back = matvec(half_matrix(OUT, 1), c1)
    fore = matvec(half_matrix(INN, 1), a1)
    c0 = [back[r] - (fore[r] + half(SRC + r, 1)) for r in range(NV)]
    for v in range(NV):
        carry[pl.ds(8 * v, NK, stride=2)] = a0[v]
        carry[pl.ds(8 * v + 1, NK, stride=2)] = a1[v]
        carry[pl.ds(8 * (NV + v), NK, stride=2)] = c0[v]
        carry[pl.ds(8 * (NV + v) + 1, NK, stride=2)] = c1[v]

    def by_step(ref, step, r):
        return [ref[pl.ds(pl.multiple_of((step * NV * NV + NV * r + c) * 8, 8), 8)] for c in range(NV)]

    def sweep_ahead(step, held):
        new = []
        for r in range(NV):
            at = pl.ds(pl.multiple_of((step * NV + r) * 8, 8), 8)
            val = residue(source[at], by_step(lows_by, step, r), held)
            ysweep[at] = val
            new.append(val)
        return tuple(new)

    lax.fori_loop(0, HALF, sweep_ahead, tuple(carry[tile_of(v)] for v in range(NV)), unroll=4)

    def sweep_back(n, held):
        step = HALF - 1 - n
        new = []
        for r in range(NV):
            at = pl.ds(pl.multiple_of((step * NV + r) * 8, 8), 8)
            val = residue(ysweep[at], by_step(upps_by, step, r), held)
            wnat[pl.ds(128 * r + step, 8, stride=HALF)] = val
            new.append(val)
        return tuple(new)

    lax.fori_loop(0, HALF, sweep_back, tuple(carry[tile_of(NV + v)] for v in range(NV)), unroll=4)

    for v in range(NV):
        turned = wnat[pl.ds(128 * v, 128)].T
        wvar[pl.ds(128 * v, 128)] = turned
        for kind, weight in enumerate((alp_v, bet_v)):
            terms = [turned[8 * t : 8 * t + 8] * weight[pl.ds(128 * v + 8 * t, 8)] for t in range(16)]
            while len(terms) > 1:
                terms = [terms[t] + terms[t + 1] for t in range(0, len(terms), 2)]
            hsend[pl.ds(NV * kind + v, 1), 0] = jnp.sum(terms[0], axis=0, keepdims=True)
    spread(hsend, hrecv, 2 * NV, 3)
    for v in range(NV):
        wt[pl.ds(v, LANES, stride=8)] = wvar[pl.ds(128 * v, 128)]

    def span_ahead(j, z):
        z = pt[at_j(j)] * wt[at_j(j)] - lt[at_j(j)] * z
        wt[at_j(j)] = z
        return z

    lax.fori_loop(0, LANES, span_ahead, zeros5, unroll=8)

    def span_back(n, z):
        j = LANES - 1 - n
        z = wt[at_j(j)] - ut[at_j(j)] * z
        wt[at_j(j)] = z
        return z

    lax.fori_loop(0, LANES, span_back, zeros5, unroll=8)

    settle(grecv, (SPAN - 1) * 3 * NV, 5)
    settle(hrecv, (SPAN - 1) * 2 * NV, 7)
    a = zeros5
    sent = []
    for d in range(SPAN):
        sentry[pl.ds(8 * d, NV)] = a
        sent.append(a)
        a = hrecv[pl.ds(2 * NV * d, NV), 0] + grecv[pl.ds(3 * NV * d, NV), 0] * a
    c = zeros5
    for d in reversed(range(SPAN)):
        sentry[pl.ds(8 * (SPAN + d), NV)] = c
        c = (
            hrecv[pl.ds(2 * NV * d + NV, NV), 0]
            + grecv[pl.ds(3 * NV * d + NV, NV), 0] * sent[d]
            + grecv[pl.ds(3 * NV * d + 2 * NV, NV), 0] * c
        )
    a_in = sentry[pl.ds(pl.multiple_of(8 * me_s, 8), NV)]
    c_in = sentry[pl.ds(pl.multiple_of(8 * (SPAN + me_s), 8), NV)]

    def close(j, _):
        wt[at_j(j)] = wt[at_j(j)] + aa[at_j(j)] * a_in + cc[at_j(j)] * c_in
        return 0

    lax.fori_loop(0, LANES, close, 0, unroll=8)

    for n in range(7, 10):
        loads[n].wait()
    for v in range(NV):
        x = wt[pl.ds(v, LANES, stride=8)].T
        held = None
        planes = []
        for k in range(NK):
            at = pl.ds(128 * v + 32 * k, 32)
            now = npn[at].astype(F32) * x[32 * k : 32 * k + 32]
            held = now if held is None else now - nln[at].astype(F32) * held
            planes.append(held)
        held = None
        for k in reversed(range(NK)):
            at = pl.ds(128 * v + 32 * k, 32)
            held = planes[k] if held is None else planes[k] - nun[at].astype(F32) * held
            out_ref[at] = held

    settle(send1, (CHORD - 1) * GROUPS, 0)
    settle(send2, (CHORD - 1) * 2, 2)
    settle(grecv, (SPAN - 1) * 3 * NV, 4)
    settle(hrecv, (SPAN - 1) * 2 * NV, 6)


def on_device(*args):
    flat = [a.reshape(-1, LANES) for a in args]
    f32 = lambda *shape: pltpu.VMEM(shape, F32)
    b16 = lambda *shape: pltpu.VMEM(shape, jnp.bfloat16)
    wide, narrow = NV * NV * 128, NV * 128
    scratch = [
        f32(narrow, LANES), b16(wide, LANES), b16(wide, LANES), b16(wide, LANES),
        f32(narrow, LANES), f32(narrow, LANES), f32(narrow, LANES),
        b16(narrow, LANES), b16(narrow, LANES), b16(narrow, LANES),
        f32(wide, LANES), f32(wide, LANES), f32(wide, LANES),
        f32(HALF * NV * 8, LANES),
        f32(88 * 8, LANES),
        f32(88 * NK, LANES),
        f32(CHORD * GROUPS, 1, LANES), f32(CHORD * GROUPS, 1, LANES),
        f32(88 * CHORD, LANES),
        f32(2 * NV * CHORD, LANES), f32(NV * CHORD, LANES),
        f32(2 * CHORD, 1, LANES), f32(2 * CHORD, 1, LANES),
        f32(64, LANES), f32(80, LANES),
        f32(HALF * NV * 8, LANES), f32(narrow, LANES),
    ]
    scratch += [f32(8 * LANES, LANES) for _ in range(10)]
    scratch += [
        f32(3 * NV, 1, LANES), f32(SPAN * 3 * NV, 1, LANES),
        f32(2 * NV, 1, LANES), f32(SPAN * 2 * NV, 1, LANES),
        f32(2 * SPAN * 8, LANES),
        f32(wide, LANES), f32(wide, LANES), f32(narrow, LANES), f32(narrow, LANES), f32(narrow, LANES),
        pltpu.SemaphoreType.DMA((10,)),
        pltpu.SemaphoreType.DMA((8,)),
    ]
    out = pl.pallas_call(
        kernel,
        out_shape=jax.ShapeDtypeStruct((narrow, LANES), F32),
        in_specs=[pl.BlockSpec(memory_space=pl.ANY)] * 10,
        out_specs=pl.BlockSpec(memory_space=pltpu.VMEM),
        scratch_shapes=scratch,
        compiler_params=pltpu.CompilerParams(
            collective_id=0, has_side_effects=True, vmem_limit_bytes=60 * 1024 * 1024
        ),
    )(*flat)
    return out.reshape(NV, NK, CELLS, LANES)


def solution(mesh):
    grid = P(None, None, "chord", "span")
    deep = P(None, None, None, "chord", "span")
    return jax.shard_map(
        on_device,
        mesh=mesh,
        in_specs=(grid, deep, deep, deep, grid, grid, grid, grid, grid, grid),
        out_specs=grid,
        check_vma=False,
    )
```

```python
import functools

import jax
import jax.numpy as jnp
from jax import lax
from jax.experimental import pallas as pl
from jax.experimental.pallas import tpu as pltpu
from jax.sharding import PartitionSpec as P

F32 = jnp.float32
MESH = pl.DeviceIdType.MESH

NV = 5
NK = 4
CHORD = 32
SPAN = 8
CELLS = 32
LANES = 128
HALF = 16
GROUPS = 11
MAT, VEC, OUT, INN, SRC = 0, 25, 30, 55, 80
ZS, XS = 8, 4


def ring(step, size):
    return min(step, size - step)


CHORD_PEERS = sorted(
    [(dz, dx) for dz in range(ZS) for dx in range(XS) if dz or dx], key=lambda p: -ring(p[0], ZS) - ring(p[1], XS)
)
SPAN_PEERS = (4, 5, 3, 2, 6, 7, 1)


def dot(lhs, rhs):
    terms = [a * b for a, b in zip(lhs, rhs)]
    while len(terms) > 1:
        terms = [terms[i] + terms[i + 1] if i + 1 < len(terms) else terms[i] for i in range(0, len(terms), 2)]
    return terms[0]


def affine(lhs, rhs, extra):
    a, b, c, d, e = [x * y for x, y in zip(lhs, rhs)]
    return ((a + b) + (c + d)) + (e + extra)


def residue(extra, lhs, rhs):
    a, b, c, d, e = [x * y for x, y in zip(lhs, rhs)]
    return (extra - e) - ((a + b) + (c + d))


def column(matrix, index):
    return [row[index] for row in matrix]


def matmul(lhs, rhs):
    cols = [column(rhs, j) for j in range(len(rhs[0]))]
    return [[dot(row, col) for col in cols] for row in lhs]


def matvec(lhs, vec):
    return [dot(row, vec) for row in lhs]


def block_transpose(tile, sub, blk):
    for d in (4, 2, 1):
        s_bit = (sub & d) != 0
        b_bit = (blk & d) != 0
        if d == 4:
            other = pltpu.roll(pltpu.roll(tile, 4, 0), 64, 1)
        else:
            up = pltpu.roll(pltpu.roll(tile, 8 - d, 0), 16 * d, 1)
            down = pltpu.roll(pltpu.roll(tile, d, 0), 128 - 16 * d, 1)
            other = jnp.where(s_bit, down, up)
        tile = jnp.where(s_bit == b_bit, tile, other)
    return tile


def kernel(
    res_h, piv_h, low_h, upp_h, sp_h, sl_h, su_h, np_h, nl_h, nu_h,
    out_ref,
    res, piv, low, upp, spn, sln, sun, npn, nln, nun,
    pivf, lowf, uppf, source, state, comb, send1, recv1, expand, expand2, entry, entry2, total,
    send2, recv2, unsh, carry, ysweep, wnat,
    wt, pt, lt, ut, gain, pre, alp, bet, cc, aa,
    gsend, grecv, hsend, hrecv, sentry,
    wvar, alp_v, bet_v,
    load_sem, sems,
):
    me_c = lax.axis_index("chord")
    me_s = lax.axis_index("span")

    z, x = me_c // XS, lax.rem(me_c, XS)

    def chord_peer(peer):
        return lax.rem(z + peer[0], ZS) * XS + lax.rem(x + peer[1], XS)

    barrier = pltpu.get_barrier_semaphore()
    for peer in CHORD_PEERS:
        pl.semaphore_signal(barrier, inc=1, device_id={"chord": chord_peer(peer)}, device_id_type=MESH)
    for o in SPAN_PEERS:
        pl.semaphore_signal(barrier, inc=1, device_id={"span": lax.rem(me_s + o, SPAN)}, device_id_type=MESH)

    loads = {}
    for n, src, dst in [
        (1, piv_h, piv), (0, res_h, res), (2, low_h, low), (3, upp_h, upp), (4, sp_h, spn), (5, sl_h, sln),
        (6, su_h, sun), (7, np_h, npn), (8, nl_h, nln), (9, nu_h, nun),
    ]:
        copy = pltpu.make_async_copy(src, dst, load_sem.at[n])
        copy.start()
        loads[n] = copy

    sub = lax.broadcasted_iota(jnp.int32, (8, LANES), 0)
    lane = lax.broadcasted_iota(jnp.int32, (8, LANES), 1)
    blk = lane // 16

    to_row = lax.broadcasted_iota(jnp.int32, (LANES, LANES), 0)
    from_row = lax.broadcasted_iota(jnp.int32, (LANES, LANES), 1)
    order = jnp.where(from_row == HALF * lax.rem(to_row, 8) + to_row // 8, 1.0, 0.0).astype(jnp.bfloat16)

    def widen(src, dst):
        def body(n, _):
            rows = pl.ds(pl.multiple_of(n * 128, 128), 128)
            dst[rows] = jnp.dot(order, src[rows], preferred_element_type=F32)
            return 0

        lax.fori_loop(0, NV * NV, body, 0, unroll=5)

    loads[1].wait()
    widen(piv, pivf)
    loads[2].wait()
    widen(low, lowf)
    loads[3].wait()
    widen(upp, uppf)
    loads[0].wait()

    zero = jnp.zeros((8, LANES), F32)

    def tile_of(value):
        return pl.ds(8 * value, 8)

    def strided(ref, index, step):
        return ref[pl.ds(index * 128 + step, 8, stride=HALF)]

    def block(ref, index, step):
        return ref[pl.ds(pl.multiple_of(index * 128 + 8 * step, 8), 8)]

    def blocks(ref, step):
        return [[block(ref, 5 * r + c, step) for c in range(NV)] for r in range(NV)]

    def sources(step):
        cells = [strided(res, c, step) for c in range(NV)]
        src = [dot([block(pivf, 5 * r + c, step) for c in range(NV)], cells) for r in range(NV)]
        for r in range(NV):
            source[pl.ds(pl.multiple_of((step * NV + r) * 8, 8), 8)] = src[r]
        return src

    def map_step(step, odd):
        src = sources(step)
        lows = blocks(lowf, step)
        cols = []
        for c in range(NV):
            new = matvec(lows, [state[tile_of(MAT + 5 * r + c)] for r in range(NV)])
            for r in range(NV):
                state[tile_of(MAT + 5 * r + c)] = new[r]
            cols.append(new)
        vec = [state[tile_of(VEC + r)] for r in range(NV)]
        new = [affine(lows[r], vec, src[r]) if odd else -residue(src[r], lows[r], vec) for r in range(NV)]
        for r in range(NV):
            state[tile_of(VEC + r)] = new[r]
        cols.append(new)
        upps = blocks(uppf, step)
        for r in range(NV):
            row = [state[tile_of(OUT + 5 * r + c)] for c in range(NV)]
            for c in range(NV):
                at = tile_of(INN + 5 * r + c)
                state[at] = affine(row, cols[c], state[at])
            at = tile_of(SRC + r)
            state[at] = affine(row, cols[NV], state[at])
            for c in range(NV):
                state[tile_of(OUT + 5 * r + c)] = dot(row, column(upps, c))

    first = sources(0)
    for r in range(NV):
        for c in range(NV):
            low = block(lowf, 5 * r + c, 0)
            state[tile_of(MAT + 5 * r + c)] = low
            state[tile_of(INN + 5 * r + c)] = low
            state[tile_of(OUT + 5 * r + c)] = block(uppf, 5 * r + c, 0)
        state[tile_of(VEC + r)] = -first[r]
        state[tile_of(SRC + r)] = -first[r]
    map_step(1, True)

    def map_pair(pair, _):
        map_step(2 * pair, False)
        map_step(2 * pair + 1, True)
        return 0

    lax.fori_loop(1, HALF // 2, map_pair, 0)

    def half(value, which):
        return state[pl.ds(8 * value + which, NK, stride=2)]

    def half_matrix(base, which):
        return [[half(base + 5 * r + c, which) for c in range(NV)] for r in range(NV)]

    def half_vector(base, which):
        return [half(base + r, which) for r in range(NV)]

    def put(value, data):
        comb[pl.ds(NK * value, NK)] = data

    mat0 = half_matrix(MAT, 0)
    vec0 = half_vector(VEC, 0)
    mat1 = half_matrix(MAT, 1)
    mats = matmul(mat1, mat0)
    vecs = matvec(mat1, vec0)
    for r in range(NV):
        for c in range(NV):
            put(MAT + 5 * r + c, mats[r][c])
        put(VEC + r, vecs[r] + half(VEC + r, 1))
    inn1 = half_matrix(INN, 1)
    part = matmul(inn1, mat0)
    tail = [t + half(SRC + r, 1) for r, t in enumerate(matvec(inn1, vec0))]
    out0 = half_matrix(OUT, 0)
    outs = matmul(out0, half_matrix(OUT, 1))
    inns = matmul(out0, part)
    srcs = matvec(out0, tail)
    for r in range(NV):
        for c in range(NV):
            put(OUT + 5 * r + c, outs[r][c])
            put(INN + 5 * r + c, inns[r][c] + half(INN + 5 * r + c, 0))
        put(SRC + r, srcs[r] + half(SRC + r, 0))
    for value in range(85, 88):
        put(value, jnp.zeros((NK, LANES), F32))

    def shuffle(k, _):
        for g in range(GROUPS):
            tile = comb[pl.ds(NK * 8 * g + k, 8, stride=NK)]
            send1[pl.ds(8 * GROUPS * k + g, 8, stride=GROUPS), 0] = block_transpose(tile, sub, blk)
        return 0

    lax.fori_loop(0, NK, shuffle, 0)

    pl.semaphore_wait(barrier, CHORD - 1 + SPAN - 1)

    def exchange(send, recv, rows, at):
        for peer in CHORD_PEERS:
            to = chord_peer(peer)
            pltpu.make_async_remote_copy(
                src_ref=send.at[pl.ds(to * rows, rows)],
                dst_ref=recv.at[pl.ds(me_c * rows, rows)],
                send_sem=sems.at[2 * at],
                recv_sem=sems.at[2 * at + 1],
                device_id={"chord": to},
                device_id_type=MESH,
            ).start()
        recv[pl.ds(me_c * rows, rows)] = send[pl.ds(me_c * rows, rows)]

    def spread(send, recv, rows, at):
        for o in SPAN_PEERS:
            pltpu.make_async_remote_copy(
                src_ref=send,
                dst_ref=recv.at[pl.ds(me_s * rows, rows)],
                send_sem=sems.at[2 * at],
                recv_sem=sems.at[2 * at + 1],
                device_id={"span": lax.rem(me_s + o, SPAN)},
                device_id_type=MESH,
            ).start()
        recv[pl.ds(me_s * rows, rows)] = send[...]

    def settle(ref, rows, sem):
        whole = ref.at[pl.ds(0, rows)]
        pltpu.make_async_copy(whole, whole, sems.at[sem]).wait()

    exchange(send1, recv1, GROUPS, 0)

    for n, (src, dst) in enumerate([(spn, pt), (sln, lt), (sun, ut)]):
        loads[4 + n].wait()
        for v in range(NV):
            dst[pl.ds(v, LANES, stride=8)] = src[pl.ds(128 * v, 128)].T

    def at_j(j):
        return pl.ds(pl.multiple_of(8 * j, 8), NV)

    ones5 = jnp.ones((NV, LANES), F32)
    zeros5 = jnp.zeros((NV, LANES), F32)

    def gains_ahead(j, held):
        g, p = held
        g = -(lt[at_j(j)] * g)
        gain[at_j(j)] = g
        pre[at_j(j)] = p
        return (g, -(ut[at_j(j)] * p))

    g_end, _ = lax.fori_loop(0, LANES, gains_ahead, (ones5, ones5), unroll=8)

    def gains_back(n, held):
        suf, b, c, a, low_next = held
        j = LANES - 1 - n
        l, u, p = lt[at_j(j)], ut[at_j(j)], pt[at_j(j)]
        alp[at_j(j)] = suf * p
        b = pre[at_j(j)] - low_next * b
        bet[at_j(j)] = b * p
        c = -(u * c)
        cc[at_j(j)] = c
        a = gain[at_j(j)] - u * a
        aa[at_j(j)] = a
        return (-(l * suf), b, c, a, l)

    _, _, c_top, a_top, _ = lax.fori_loop(
        0, LANES, gains_back, (ones5, zeros5, ones5, zeros5, zeros5), unroll=8
    )
    gsend[pl.ds(0, NV), 0] = g_end
    gsend[pl.ds(NV, NV), 0] = a_top
    gsend[pl.ds(2 * NV, NV), 0] = c_top
    spread(gsend, grecv, 3 * NV, 2)
    for v in range(NV):
        alp_v[pl.ds(128 * v, 128)] = alp[pl.ds(v, LANES, stride=8)]
        bet_v[pl.ds(128 * v, 128)] = bet[pl.ds(v, LANES, stride=8)]

    settle(recv1, (CHORD - 1) * GROUPS, 1)

    ahead_values = 8 * (OUT // 8 + 1)

    def unpack(q, groups):
        for g in groups:
            tile = recv1[pl.ds(8 * GROUPS * q + g, 8, stride=GROUPS), 0]
            for s in range(8):
                value = 8 * g + s
                if value < 85:
                    moved = tile if s == 0 else pltpu.roll(tile, LANES - 16 * s, 1)
                    if value < ahead_values:
                        expand[pl.ds(pl.multiple_of(CHORD * value + 8 * q, 8), 8)] = moved
                    if value >= OUT:
                        expand2[pl.ds(pl.multiple_of(CHORD * (value - OUT) + 8 * q, 8), 8)] = moved

    def row(value, at):
        return expand[pl.ds(CHORD * value + at, 1)]

    def row2(value, at):
        return expand2[pl.ds(CHORD * (value - OUT) + at, 1)]

    def tile2(value, q):
        return expand2[pl.ds(pl.multiple_of(CHORD * (value - OUT) + 8 * q, 8), 8)]

    def relay_ahead(q, held):
        for n in range(8):
            at = 8 * q + n
            new = []
            for c in range(NV):
                entry[pl.ds(CHORD * c + at, 1)] = held[c]
            for r in range(NV):
                new.append(affine([row(MAT + 5 * r + c, at) for c in range(NV)], held, row(VEC + r, at)))
            held = new
        return held

    held = [jnp.zeros((1, LANES), F32) for _ in range(NV)]
    for q in range(CHORD // 8):
        unpack(q, range(ahead_values // 8))
    for q in range(CHORD // 8):
        held = relay_ahead(q, held)
        unpack(q, range(ahead_values // 8, GROUPS))

    for q in range(CHORD // 8):
        vec = [entry[pl.ds(CHORD * c + 8 * q, 8)] for c in range(NV)]
        for r in range(NV):
            mats_r = [tile2(INN + 5 * r + c, q) for c in range(NV)]
            total[pl.ds(CHORD * r + 8 * q, 8)] = -affine(mats_r, vec, tile2(SRC + r, q))

    def relay_back(q, held):
        for n in reversed(range(8)):
            at = 8 * q + n
            new = []
            for c in range(NV):
                entry2[pl.ds(CHORD * c + at, 1)] = held[c]
            for r in range(NV):
                new.append(
                    affine([row2(OUT + 5 * r + c, at) for c in range(NV)], held, total[pl.ds(CHORD * r + at, 1)])
                )
            held = new
        return held

    held = [jnp.zeros((1, LANES), F32) for _ in range(NV)]
    for q in reversed(range(CHORD // 8)):
        held = relay_back(q, held)

    for q in range(CHORD // 8):
        for kind in range(2):
            tile = zero
            for s in range(NV):
                part_s = (entry2 if kind else entry)[pl.ds(CHORD * s + 8 * q, 8)]
                if s > 0:
                    part_s = pltpu.roll(part_s, 16 * s, 1)
                tile = jnp.where(blk == s, part_s, tile)
            send2[pl.ds(16 * q + kind, 8, stride=2), 0] = tile

    exchange(send2, recv2, 2, 1)

    settle(recv2, (CHORD - 1) * 2, 3)

    for kind in range(2):
        for k in range(NK):
            tile = recv2[pl.ds(16 * k + kind, 8, stride=2), 0]
            unsh[pl.ds(8 * (NK * kind + k), 8)] = block_transpose(tile, sub, blk)
    a0 = [unsh[pl.ds(v, NK, stride=8)] for v in range(NV)]
    c1 = [unsh[pl.ds(8 * NK + v, NK, stride=8)] for v in range(NV)]
    a1 = [m + half(VEC + r, 0) for r, m in enumerate(matvec(half_matrix(MAT, 0), a0))]
    back = matvec(half_matrix(OUT, 1), c1)
    fore = matvec(half_matrix(INN, 1), a1)
    c0 = [back[r] - (fore[r] + half(SRC + r, 1)) for r in range(NV)]
    for v in range(NV):
        carry[pl.ds(8 * v, NK, stride=2)] = a0[v]
        carry[pl.ds(8 * v + 1, NK, stride=2)] = a1[v]
        carry[pl.ds(8 * (NV + v), NK, stride=2)] = c0[v]
        carry[pl.ds(8 * (NV + v) + 1, NK, stride=2)] = c1[v]

    def by_step(ref, step, r):
        return [block(ref, NV * r + c, step) for c in range(NV)]

    def sweep_ahead(step, held):
        new = []
        for r in range(NV):
            at = pl.ds(pl.multiple_of((step * NV + r) * 8, 8), 8)
            val = residue(source[at], by_step(lowf, step, r), held)
            ysweep[at] = val
            new.append(val)
        return tuple(new)

    lax.fori_loop(0, HALF, sweep_ahead, tuple(carry[tile_of(v)] for v in range(NV)), unroll=4)

    def sweep_back(n, held):
        step = HALF - 1 - n
        new = []
        for r in range(NV):
            at = pl.ds(pl.multiple_of((step * NV + r) * 8, 8), 8)
            val = residue(ysweep[at], by_step(uppf, step, r), held)
            wnat[pl.ds(128 * r + step, 8, stride=HALF)] = val
            new.append(val)
        return tuple(new)

    lax.fori_loop(0, HALF, sweep_back, tuple(carry[tile_of(NV + v)] for v in range(NV)), unroll=4)

    for v in range(NV):
        turned = wnat[pl.ds(128 * v, 128)].T
        wvar[pl.ds(128 * v, 128)] = turned
        for kind, weight in enumerate((alp_v, bet_v)):
            terms = [turned[8 * t : 8 * t + 8] * weight[pl.ds(128 * v + 8 * t, 8)] for t in range(16)]
            while len(terms) > 1:
                terms = [terms[t] + terms[t + 1] for t in range(0, len(terms), 2)]
            hsend[pl.ds(NV * kind + v, 1), 0] = jnp.sum(terms[0], axis=0, keepdims=True)
    spread(hsend, hrecv, 2 * NV, 3)
    for v in range(NV):
        wt[pl.ds(v, LANES, stride=8)] = wvar[pl.ds(128 * v, 128)]

    def span_ahead(j, z):
        z = pt[at_j(j)] * wt[at_j(j)] - lt[at_j(j)] * z
        wt[at_j(j)] = z
        return z

    lax.fori_loop(0, LANES, span_ahead, zeros5, unroll=8)

    def span_back(n, z):
        j = LANES - 1 - n
        z = wt[at_j(j)] - ut[at_j(j)] * z
        wt[at_j(j)] = z
        return z

    lax.fori_loop(0, LANES, span_back, zeros5, unroll=8)

    settle(grecv, (SPAN - 1) * 3 * NV, 5)
    settle(hrecv, (SPAN - 1) * 2 * NV, 7)
    a = zeros5
    sent = []
    for d in range(SPAN):
        sentry[pl.ds(8 * d, NV)] = a
        sent.append(a)
        a = hrecv[pl.ds(2 * NV * d, NV), 0] + grecv[pl.ds(3 * NV * d, NV), 0] * a
    c = zeros5
    for d in reversed(range(SPAN)):
        sentry[pl.ds(8 * (SPAN + d), NV)] = c
        c = (
            hrecv[pl.ds(2 * NV * d + NV, NV), 0]
            + grecv[pl.ds(3 * NV * d + NV, NV), 0] * sent[d]
            + grecv[pl.ds(3 * NV * d + 2 * NV, NV), 0] * c
        )
    a_in = sentry[pl.ds(pl.multiple_of(8 * me_s, 8), NV)]
    c_in = sentry[pl.ds(pl.multiple_of(8 * (SPAN + me_s), 8), NV)]

    def close(j, _):
        wt[at_j(j)] = wt[at_j(j)] + aa[at_j(j)] * a_in + cc[at_j(j)] * c_in
        return 0

    lax.fori_loop(0, LANES, close, 0, unroll=8)

    for n in range(7, 10):
        loads[n].wait()
    for v in range(NV):
        x = wt[pl.ds(v, LANES, stride=8)].T
        held = None
        planes = []
        for k in range(NK):
            at = pl.ds(128 * v + 32 * k, 32)
            now = npn[at].astype(F32) * x[32 * k : 32 * k + 32]
            held = now if held is None else now - nln[at].astype(F32) * held
            planes.append(held)
        held = None
        for k in reversed(range(NK)):
            at = pl.ds(128 * v + 32 * k, 32)
            held = planes[k] if held is None else planes[k] - nun[at].astype(F32) * held
            out_ref[at] = held

    settle(send1, (CHORD - 1) * GROUPS, 0)
    settle(send2, (CHORD - 1) * 2, 2)
    settle(grecv, (SPAN - 1) * 3 * NV, 4)
    settle(hrecv, (SPAN - 1) * 2 * NV, 6)


def on_device(*args):
    flat = [a.reshape(-1, LANES) for a in args]
    f32 = lambda *shape: pltpu.VMEM(shape, F32)
    b16 = lambda *shape: pltpu.VMEM(shape, jnp.bfloat16)
    wide, narrow = NV * NV * 128, NV * 128
    scratch = [
        f32(narrow, LANES), b16(wide, LANES), b16(wide, LANES), b16(wide, LANES),
        f32(narrow, LANES), f32(narrow, LANES), f32(narrow, LANES),
        b16(narrow, LANES), b16(narrow, LANES), b16(narrow, LANES),
        f32(wide, LANES), f32(wide, LANES), f32(wide, LANES),
        f32(HALF * NV * 8, LANES),
        f32(88 * 8, LANES),
        f32(88 * NK, LANES),
        f32(CHORD * GROUPS, 1, LANES), f32(CHORD * GROUPS, 1, LANES),
        f32(32 * CHORD, LANES), f32(55 * CHORD, LANES),
        f32(NV * CHORD, LANES), f32(NV * CHORD, LANES), f32(NV * CHORD, LANES),
        f32(2 * CHORD, 1, LANES), f32(2 * CHORD, 1, LANES),
        f32(64, LANES), f32(80, LANES),
        f32(HALF * NV * 8, LANES), f32(narrow, LANES),
    ]
    scratch += [f32(8 * LANES, LANES) for _ in range(10)]
    scratch += [
        f32(3 * NV, 1, LANES), f32(SPAN * 3 * NV, 1, LANES),
        f32(2 * NV, 1, LANES), f32(SPAN * 2 * NV, 1, LANES),
        f32(2 * SPAN * 8, LANES),
        f32(narrow, LANES), f32(narrow, LANES), f32(narrow, LANES),
        pltpu.SemaphoreType.DMA((10,)),
        pltpu.SemaphoreType.DMA((8,)),
    ]
    out = pl.pallas_call(
        kernel,
        out_shape=pltpu.VMEM((narrow, LANES), F32),
        in_specs=[pl.BlockSpec(memory_space=pl.ANY)] * 10,
        out_specs=pl.BlockSpec(memory_space=pltpu.VMEM),
        scratch_shapes=scratch,
        compiler_params=pltpu.CompilerParams(
            collective_id=0, has_side_effects=True, vmem_limit_bytes=60 * 1024 * 1024
        ),
    )(*flat)
    return out.reshape(NV, NK, CELLS, LANES)


def solution(mesh):
    grid = P(None, None, "chord", "span")
    deep = P(None, None, None, "chord", "span")
    return jax.shard_map(
        on_device,
        mesh=mesh,
        in_specs=(grid, deep, deep, deep, grid, grid, grid, grid, grid, grid),
        out_specs=grid,
        check_vma=False,
    )
```

```python
import functools

import jax
import jax.numpy as jnp
from jax import lax
from jax.experimental import pallas as pl
from jax.experimental.pallas import tpu as pltpu
from jax.sharding import PartitionSpec as P

F32 = jnp.float32
MESH = pl.DeviceIdType.MESH

NV = 5
NK = 4
CHORD = 32
SPAN = 8
CELLS = 32
LANES = 128
HALF = 16
GROUPS = 11
MAT, VEC, OUT, INN, SRC = 0, 25, 30, 55, 80
ZS, XS = 8, 4


def ring(step, size):
    return min(step, size - step)


CHORD_PEERS = sorted(
    [(dz, dx) for dz in range(ZS) for dx in range(XS) if dz or dx], key=lambda p: -ring(p[0], ZS) - ring(p[1], XS)
)
SPAN_PEERS = (4, 5, 3, 2, 6, 7, 1)


def dot(lhs, rhs):
    terms = [a * b for a, b in zip(lhs, rhs)]
    while len(terms) > 1:
        terms = [terms[i] + terms[i + 1] if i + 1 < len(terms) else terms[i] for i in range(0, len(terms), 2)]
    return terms[0]


def affine(lhs, rhs, extra):
    a, b, c, d, e = [x * y for x, y in zip(lhs, rhs)]
    return ((a + b) + (c + d)) + (e + extra)


def residue(extra, lhs, rhs):
    a, b, c, d, e = [x * y for x, y in zip(lhs, rhs)]
    return (extra - e) - ((a + b) + (c + d))


def column(matrix, index):
    return [row[index] for row in matrix]


def matmul(lhs, rhs):
    cols = [column(rhs, j) for j in range(len(rhs[0]))]
    return [[dot(row, col) for col in cols] for row in lhs]


def matvec(lhs, vec):
    return [dot(row, vec) for row in lhs]


def block_transpose(tile, sub, blk):
    for d in (4, 2, 1):
        s_bit = (sub & d) != 0
        b_bit = (blk & d) != 0
        if d == 4:
            other = pltpu.roll(pltpu.roll(tile, 4, 0), 64, 1)
        else:
            up = pltpu.roll(pltpu.roll(tile, 8 - d, 0), 16 * d, 1)
            down = pltpu.roll(pltpu.roll(tile, d, 0), 128 - 16 * d, 1)
            other = jnp.where(s_bit, down, up)
        tile = jnp.where(s_bit == b_bit, tile, other)
    return tile


def skewed_transpose(tile, blk):
    tile = pltpu.roll(tile, 0, 1, stride=16, stride_axis=0)
    for d in (1, 2, 4):
        tile = jnp.where((blk & d) != 0, pltpu.roll(tile, 8 - d, 0), tile)
    return pltpu.roll(tile, 0, 1, stride=16, stride_axis=0)


def kernel(
    res_h, piv_h, low_h, upp_h, sp_h, sl_h, su_h, np_h, nl_h, nu_h,
    out_ref,
    res, piv, low, upp, spn, sln, sun, npn, nln, nun,
    pivf, lowf, uppf, source, state, comb, send1, recv1, expand, expand2, entry, entry2, total,
    send2, recv2, unsh, carry, ysweep, wnat,
    wt, pt, lt, ut, gain, pre, alp, bet, cc, aa,
    gsend, grecv, hsend, hrecv, sentry,
    wvar, alp_v, bet_v,
    load_sem, sems,
):
    me_c = lax.axis_index("chord")
    me_s = lax.axis_index("span")

    z, x = me_c // XS, lax.rem(me_c, XS)

    def chord_peer(peer):
        return lax.rem(z + peer[0], ZS) * XS + lax.rem(x + peer[1], XS)

    barrier = pltpu.get_barrier_semaphore()
    for peer in CHORD_PEERS:
        pl.semaphore_signal(barrier, inc=1, device_id={"chord": chord_peer(peer)}, device_id_type=MESH)
    for o in SPAN_PEERS:
        pl.semaphore_signal(barrier, inc=1, device_id={"span": lax.rem(me_s + o, SPAN)}, device_id_type=MESH)

    loads = {}
    for n, src, dst in [
        (1, piv_h, piv), (0, res_h, res), (2, low_h, low), (3, upp_h, upp), (4, sp_h, spn), (5, sl_h, sln),
        (6, su_h, sun), (7, np_h, npn), (8, nl_h, nln), (9, nu_h, nun),
    ]:
        copy = pltpu.make_async_copy(src, dst, load_sem.at[n])
        copy.start()
        loads[n] = copy

    sub = lax.broadcasted_iota(jnp.int32, (8, LANES), 0)
    lane = lax.broadcasted_iota(jnp.int32, (8, LANES), 1)
    blk = lane // 16

    to_row = lax.broadcasted_iota(jnp.int32, (LANES, LANES), 0)
    from_row = lax.broadcasted_iota(jnp.int32, (LANES, LANES), 1)
    order = jnp.where(from_row == HALF * lax.rem(to_row, 8) + to_row // 8, 1.0, 0.0).astype(jnp.bfloat16)

    def widen(src, dst):
        def body(n, _):
            rows = pl.ds(pl.multiple_of(n * 128, 128), 128)
            dst[rows] = jnp.dot(order, src[rows], preferred_element_type=F32)
            return 0

        lax.fori_loop(0, NV * NV, body, 0, unroll=5)

    loads[1].wait()
    widen(piv, pivf)
    loads[2].wait()
    widen(low, lowf)
    loads[3].wait()
    widen(upp, uppf)
    loads[0].wait()

    zero = jnp.zeros((8, LANES), F32)

    def tile_of(value):
        return pl.ds(8 * value, 8)

    def strided(ref, index, step):
        return ref[pl.ds(index * 128 + step, 8, stride=HALF)]

    def block(ref, index, step):
        return ref[pl.ds(pl.multiple_of(index * 128 + 8 * step, 8), 8)]

    def blocks(ref, step):
        return [[block(ref, 5 * r + c, step) for c in range(NV)] for r in range(NV)]

    def sources(step):
        cells = [strided(res, c, step) for c in range(NV)]
        src = [dot([block(pivf, 5 * r + c, step) for c in range(NV)], cells) for r in range(NV)]
        for r in range(NV):
            source[pl.ds(pl.multiple_of((step * NV + r) * 8, 8), 8)] = src[r]
        return src

    def map_step(step, odd):
        src = sources(step)
        lows = blocks(lowf, step)
        cols = []
        for c in range(NV):
            new = matvec(lows, [state[tile_of(MAT + 5 * r + c)] for r in range(NV)])
            for r in range(NV):
                state[tile_of(MAT + 5 * r + c)] = new[r]
            cols.append(new)
        vec = [state[tile_of(VEC + r)] for r in range(NV)]
        new = [affine(lows[r], vec, src[r]) if odd else -residue(src[r], lows[r], vec) for r in range(NV)]
        for r in range(NV):
            state[tile_of(VEC + r)] = new[r]
        cols.append(new)
        upps = blocks(uppf, step)
        for r in range(NV):
            row = [state[tile_of(OUT + 5 * r + c)] for c in range(NV)]
            for c in range(NV):
                at = tile_of(INN + 5 * r + c)
                state[at] = affine(row, cols[c], state[at])
            at = tile_of(SRC + r)
            state[at] = affine(row, cols[NV], state[at])
            for c in range(NV):
                state[tile_of(OUT + 5 * r + c)] = dot(row, column(upps, c))

    first = sources(0)
    for r in range(NV):
        for c in range(NV):
            low = block(lowf, 5 * r + c, 0)
            state[tile_of(MAT + 5 * r + c)] = low
            state[tile_of(INN + 5 * r + c)] = low
            state[tile_of(OUT + 5 * r + c)] = block(uppf, 5 * r + c, 0)
        state[tile_of(VEC + r)] = -first[r]
        state[tile_of(SRC + r)] = -first[r]
    map_step(1, True)

    def map_pair(pair, _):
        map_step(2 * pair, False)
        map_step(2 * pair + 1, True)
        return 0

    lax.fori_loop(1, HALF // 2, map_pair, 0)

    def half(value, which):
        return state[pl.ds(8 * value + which, NK, stride=2)]

    def half_matrix(base, which):
        return [[half(base + 5 * r + c, which) for c in range(NV)] for r in range(NV)]

    def half_vector(base, which):
        return [half(base + r, which) for r in range(NV)]

    def put(value, data):
        comb[pl.ds(NK * value, NK)] = data

    mat0 = half_matrix(MAT, 0)
    vec0 = half_vector(VEC, 0)
    mat1 = half_matrix(MAT, 1)
    mats = matmul(mat1, mat0)
    vecs = matvec(mat1, vec0)
    for r in range(NV):
        for c in range(NV):
            put(MAT + 5 * r + c, mats[r][c])
        put(VEC + r, vecs[r] + half(VEC + r, 1))
    inn1 = half_matrix(INN, 1)
    part = matmul(inn1, mat0)
    tail = [t + half(SRC + r, 1) for r, t in enumerate(matvec(inn1, vec0))]
    out0 = half_matrix(OUT, 0)
    outs = matmul(out0, half_matrix(OUT, 1))
    inns = matmul(out0, part)
    srcs = matvec(out0, tail)
    for r in range(NV):
        for c in range(NV):
            put(OUT + 5 * r + c, outs[r][c])
            put(INN + 5 * r + c, inns[r][c] + half(INN + 5 * r + c, 0))
        put(SRC + r, srcs[r] + half(SRC + r, 0))
    for value in range(85, 88):
        put(value, jnp.zeros((NK, LANES), F32))

    def shuffle(k):
        for g in range(GROUPS):
            tile = comb[pl.ds(NK * 8 * g + k, 8, stride=NK)]
            send1[pl.ds(8 * GROUPS * k + g, 8, stride=GROUPS), 0] = skewed_transpose(tile, blk)

    for k in range(NK):
        shuffle(k)

    pl.semaphore_wait(barrier, CHORD - 1 + SPAN - 1)

    def exchange(send, recv, rows, at, slot):
        for peer in CHORD_PEERS:
            to = chord_peer(peer)
            pltpu.make_async_remote_copy(
                src_ref=send.at[pl.ds(to * rows, rows)],
                dst_ref=recv.at[pl.ds(slot * rows, rows)],
                send_sem=sems.at[2 * at],
                recv_sem=sems.at[2 * at + 1],
                device_id={"chord": to},
                device_id_type=MESH,
            ).start()
        recv[pl.ds(slot * rows, rows)] = send[pl.ds(me_c * rows, rows)]

    def spread(send, recv, rows, at):
        for o in SPAN_PEERS:
            pltpu.make_async_remote_copy(
                src_ref=send,
                dst_ref=recv.at[pl.ds(me_s * rows, rows)],
                send_sem=sems.at[2 * at],
                recv_sem=sems.at[2 * at + 1],
                device_id={"span": lax.rem(me_s + o, SPAN)},
                device_id_type=MESH,
            ).start()
        recv[pl.ds(me_s * rows, rows)] = send[...]

    def settle(ref, rows, sem):
        whole = ref.at[pl.ds(0, rows)]
        pltpu.make_async_copy(whole, whole, sems.at[sem]).wait()

    exchange(send1, recv1, GROUPS, 0, me_c)

    for n, (src, dst) in enumerate([(spn, pt), (sln, lt), (sun, ut)]):
        loads[4 + n].wait()
        for v in range(NV):
            dst[pl.ds(v, LANES, stride=8)] = src[pl.ds(128 * v, 128)].T

    def at_j(j):
        return pl.ds(pl.multiple_of(8 * j, 8), NV)

    ones5 = jnp.ones((NV, LANES), F32)
    zeros5 = jnp.zeros((NV, LANES), F32)

    def gains_ahead(j, held):
        g, p = held
        g = -(lt[at_j(j)] * g)
        gain[at_j(j)] = g
        pre[at_j(j)] = p
        return (g, -(ut[at_j(j)] * p))

    g_end, _ = lax.fori_loop(0, LANES, gains_ahead, (ones5, ones5), unroll=8)

    def gains_back(n, held):
        suf, b, c, a, low_next = held
        j = LANES - 1 - n
        l, u, p = lt[at_j(j)], ut[at_j(j)], pt[at_j(j)]
        alp[at_j(j)] = suf * p
        b = pre[at_j(j)] - low_next * b
        bet[at_j(j)] = b * p
        c = -(u * c)
        cc[at_j(j)] = c
        a = gain[at_j(j)] - u * a
        aa[at_j(j)] = a
        return (-(l * suf), b, c, a, l)

    _, _, c_top, a_top, _ = lax.fori_loop(
        0, LANES, gains_back, (ones5, zeros5, ones5, zeros5, zeros5), unroll=8
    )
    gsend[pl.ds(0, NV), 0] = g_end
    gsend[pl.ds(NV, NV), 0] = a_top
    gsend[pl.ds(2 * NV, NV), 0] = c_top
    spread(gsend, grecv, 3 * NV, 2)
    for v in range(NV):
        alp_v[pl.ds(128 * v, 128)] = alp[pl.ds(v, LANES, stride=8)]
        bet_v[pl.ds(128 * v, 128)] = bet[pl.ds(v, LANES, stride=8)]

    settle(recv1, (CHORD - 1) * GROUPS, 1)

    ahead_values = 8 * (OUT // 8 + 1)

    def unpack(q, groups):
        for g in groups:
            tile = recv1[pl.ds(8 * GROUPS * q + g, 8, stride=GROUPS), 0]
            for s in range(8):
                value = 8 * g + s
                if value < 85:
                    moved = tile if s == 0 else pltpu.roll(tile, LANES - 16 * s, 1)
                    if value < ahead_values:
                        expand[pl.ds(pl.multiple_of(CHORD * value + 8 * q, 8), 8)] = moved
                    if value >= OUT:
                        expand2[pl.ds(pl.multiple_of(CHORD * (value - OUT) + 8 * q, 8), 8)] = moved

    def row(value, at):
        return expand[pl.ds(CHORD * value + at, 1)]

    def row2(value, at):
        return expand2[pl.ds(CHORD * (value - OUT) + at, 1)]

    def tile2(value, q):
        return expand2[pl.ds(pl.multiple_of(CHORD * (value - OUT) + 8 * q, 8), 8)]

    def relay_ahead(q, held):
        for n in range(8):
            at = 8 * q + n
            new = []
            for c in range(NV):
                entry[pl.ds(CHORD * c + at, 1)] = held[c]
            for r in range(NV):
                new.append(affine([row(MAT + 5 * r + c, at) for c in range(NV)], held, row(VEC + r, at)))
            held = new
        return held

    held = [jnp.zeros((1, LANES), F32) for _ in range(NV)]
    for q in range(CHORD // 8):
        unpack(q, range(ahead_values // 8))
    for q in range(CHORD // 8):
        held = relay_ahead(q, held)
        unpack(q, range(ahead_values // 8, GROUPS))

    for q in range(CHORD // 8):
        vec = [entry[pl.ds(CHORD * c + 8 * q, 8)] for c in range(NV)]
        for r in range(NV):
            mats_r = [tile2(INN + 5 * r + c, q) for c in range(NV)]
            total[pl.ds(CHORD * r + 8 * q, 8)] = -affine(mats_r, vec, tile2(SRC + r, q))

    def relay_back(q, held):
        for n in reversed(range(8)):
            at = 8 * q + n
            new = []
            for c in range(NV):
                entry2[pl.ds(CHORD * c + at, 1)] = held[c]
            for r in range(NV):
                new.append(
                    affine([row2(OUT + 5 * r + c, at) for c in range(NV)], held, total[pl.ds(CHORD * r + at, 1)])
                )
            held = new
        return held

    held = [jnp.zeros((1, LANES), F32) for _ in range(NV)]
    for q in reversed(range(CHORD // 8)):
        held = relay_back(q, held)

    for q in range(CHORD // 8):
        for kind in range(2):
            tile = zero
            for s in range(NV):
                part_s = (entry2 if kind else entry)[pl.ds(CHORD * s + 8 * q, 8)]
                if s > 0:
                    part_s = pltpu.roll(part_s, 16 * s, 1)
                tile = jnp.where(blk == s, part_s, tile)
            send2[pl.ds(16 * q + kind, 8, stride=2), 0] = tile

    exchange(send2, recv2, 2, 1, me_c // 8 * 8 + lax.rem(8 - lax.rem(me_c, 8), 8))

    settle(recv2, (CHORD - 1) * 2, 3)

    for kind in range(2):
        for k in range(NK):
            tile = recv2[pl.ds(16 * k + kind, 8, stride=2), 0]
            unsh[pl.ds(8 * (NK * kind + k), 8)] = block_transpose(tile, sub, blk)
    a0 = [unsh[pl.ds(v, NK, stride=8)] for v in range(NV)]
    c1 = [unsh[pl.ds(8 * NK + v, NK, stride=8)] for v in range(NV)]
    a1 = [m + half(VEC + r, 0) for r, m in enumerate(matvec(half_matrix(MAT, 0), a0))]
    back = matvec(half_matrix(OUT, 1), c1)
    fore = matvec(half_matrix(INN, 1), a1)
    c0 = [back[r] - (fore[r] + half(SRC + r, 1)) for r in range(NV)]
    for v in range(NV):
        carry[pl.ds(8 * v, NK, stride=2)] = a0[v]
        carry[pl.ds(8 * v + 1, NK, stride=2)] = a1[v]
        carry[pl.ds(8 * (NV + v), NK, stride=2)] = c0[v]
        carry[pl.ds(8 * (NV + v) + 1, NK, stride=2)] = c1[v]

    def by_step(ref, step, r):
        return [block(ref, NV * r + c, step) for c in range(NV)]

    def sweep_ahead(step, held):
        new = []
        for r in range(NV):
            at = pl.ds(pl.multiple_of((step * NV + r) * 8, 8), 8)
            val = residue(source[at], by_step(lowf, step, r), held)
            ysweep[at] = val
            new.append(val)
        return tuple(new)

    lax.fori_loop(0, HALF, sweep_ahead, tuple(carry[tile_of(v)] for v in range(NV)), unroll=16)

    def sweep_back(n, held):
        step = HALF - 1 - n
        new = []
        for r in range(NV):
            at = pl.ds(pl.multiple_of((step * NV + r) * 8, 8), 8)
            val = residue(ysweep[at], by_step(uppf, step, r), held)
            wnat[pl.ds(128 * r + step, 8, stride=HALF)] = val
            new.append(val)
        return tuple(new)

    lax.fori_loop(0, HALF, sweep_back, tuple(carry[tile_of(NV + v)] for v in range(NV)), unroll=16)

    for v in range(NV):
        turned = wnat[pl.ds(128 * v, 128)].T
        wvar[pl.ds(128 * v, 128)] = turned
        for kind, weight in enumerate((alp_v, bet_v)):
            terms = [turned[8 * t : 8 * t + 8] * weight[pl.ds(128 * v + 8 * t, 8)] for t in range(16)]
            while len(terms) > 1:
                terms = [terms[t] + terms[t + 1] for t in range(0, len(terms), 2)]
            hsend[pl.ds(NV * kind + v, 1), 0] = jnp.sum(terms[0], axis=0, keepdims=True)
    spread(hsend, hrecv, 2 * NV, 3)
    for v in range(NV):
        wt[pl.ds(v, LANES, stride=8)] = wvar[pl.ds(128 * v, 128)]

    def span_ahead(j, z):
        z = pt[at_j(j)] * wt[at_j(j)] - lt[at_j(j)] * z
        wt[at_j(j)] = z
        return z

    lax.fori_loop(0, LANES, span_ahead, zeros5, unroll=8)

    def span_back(n, z):
        j = LANES - 1 - n
        z = wt[at_j(j)] - ut[at_j(j)] * z
        wt[at_j(j)] = z
        return z

    lax.fori_loop(0, LANES, span_back, zeros5, unroll=8)

    settle(grecv, (SPAN - 1) * 3 * NV, 5)
    settle(hrecv, (SPAN - 1) * 2 * NV, 7)
    a = zeros5
    sent = []
    for d in range(SPAN):
        sentry[pl.ds(8 * d, NV)] = a
        sent.append(a)
        a = hrecv[pl.ds(2 * NV * d, NV), 0] + grecv[pl.ds(3 * NV * d, NV), 0] * a
    c = zeros5
    for d in reversed(range(SPAN)):
        sentry[pl.ds(8 * (SPAN + d), NV)] = c
        c = (
            hrecv[pl.ds(2 * NV * d + NV, NV), 0]
            + grecv[pl.ds(3 * NV * d + NV, NV), 0] * sent[d]
            + grecv[pl.ds(3 * NV * d + 2 * NV, NV), 0] * c
        )
    a_in = sentry[pl.ds(pl.multiple_of(8 * me_s, 8), NV)]
    c_in = sentry[pl.ds(pl.multiple_of(8 * (SPAN + me_s), 8), NV)]

    def close(j, _):
        wt[at_j(j)] = wt[at_j(j)] + aa[at_j(j)] * a_in + cc[at_j(j)] * c_in
        return 0

    lax.fori_loop(0, LANES, close, 0, unroll=32)

    for n in range(7, 10):
        loads[n].wait()
    for v in range(NV):
        x = wt[pl.ds(v, LANES, stride=8)].T
        held = None
        planes = []
        for k in range(NK):
            at = pl.ds(128 * v + 32 * k, 32)
            now = npn[at].astype(F32) * x[32 * k : 32 * k + 32]
            held = now if held is None else now - nln[at].astype(F32) * held
            planes.append(held)
        held = None
        for k in reversed(range(NK)):
            at = pl.ds(128 * v + 32 * k, 32)
            held = planes[k] if held is None else planes[k] - nun[at].astype(F32) * held
            out_ref[at] = held

    settle(send1, (CHORD - 1) * GROUPS, 0)
    settle(send2, (CHORD - 1) * 2, 2)
    settle(grecv, (SPAN - 1) * 3 * NV, 4)
    settle(hrecv, (SPAN - 1) * 2 * NV, 6)


def on_device(*args):
    flat = [a.reshape(-1, LANES) for a in args]
    f32 = lambda *shape: pltpu.VMEM(shape, F32)
    b16 = lambda *shape: pltpu.VMEM(shape, jnp.bfloat16)
    wide, narrow = NV * NV * 128, NV * 128
    scratch = [
        f32(narrow, LANES), b16(wide, LANES), b16(wide, LANES), b16(wide, LANES),
        f32(narrow, LANES), f32(narrow, LANES), f32(narrow, LANES),
        b16(narrow, LANES), b16(narrow, LANES), b16(narrow, LANES),
        f32(wide, LANES), f32(wide, LANES), f32(wide, LANES),
        f32(HALF * NV * 8, LANES),
        f32(88 * 8, LANES),
        f32(88 * NK, LANES),
        f32(CHORD * GROUPS, 1, LANES), f32(CHORD * GROUPS, 1, LANES),
        f32(32 * CHORD, LANES), f32(55 * CHORD, LANES),
        f32(NV * CHORD, LANES), f32(NV * CHORD, LANES), f32(NV * CHORD, LANES),
        f32(2 * CHORD, 1, LANES), f32(2 * CHORD, 1, LANES),
        f32(64, LANES), f32(80, LANES),
        f32(HALF * NV * 8, LANES), f32(narrow, LANES),
    ]
    scratch += [f32(8 * LANES, LANES) for _ in range(10)]
    scratch += [
        f32(3 * NV, 1, LANES), f32(SPAN * 3 * NV, 1, LANES),
        f32(2 * NV, 1, LANES), f32(SPAN * 2 * NV, 1, LANES),
        f32(2 * SPAN * 8, LANES),
        f32(narrow, LANES), f32(narrow, LANES), f32(narrow, LANES),
        pltpu.SemaphoreType.DMA((10,)),
        pltpu.SemaphoreType.DMA((8,)),
    ]
    out = pl.pallas_call(
        kernel,
        out_shape=pltpu.VMEM((narrow, LANES), F32),
        in_specs=[pl.BlockSpec(memory_space=pl.ANY)] * 10,
        out_specs=pl.BlockSpec(memory_space=pltpu.VMEM),
        scratch_shapes=scratch,
        compiler_params=pltpu.CompilerParams(
            collective_id=0, has_side_effects=True, vmem_limit_bytes=60 * 1024 * 1024
        ),
    )(*flat)
    return out.reshape(NV, NK, CELLS, LANES)


def solution(mesh):
    grid = P(None, None, "chord", "span")
    deep = P(None, None, None, "chord", "span")
    return jax.shard_map(
        on_device,
        mesh=mesh,
        in_specs=(grid, deep, deep, deep, grid, grid, grid, grid, grid, grid),
        out_specs=grid,
        check_vma=False,
    )
```

```python
import functools

import jax
import jax.numpy as jnp
from jax import lax
from jax.experimental import pallas as pl
from jax.experimental.pallas import tpu as pltpu
from jax.sharding import PartitionSpec as P

F32 = jnp.float32
MESH = pl.DeviceIdType.MESH

NV = 5
NK = 4
CHORD = 32
SPAN = 8
CELLS = 32
LANES = 128
HALF = 16
GROUPS = 11
MAT, VEC, OUT, INN, SRC = 0, 25, 30, 55, 80
ZS, XS = 8, 4
WIDE = NV * NV * 128


def ring(step, size):
    return min(step, size - step)


CHORD_PEERS = sorted(
    [(dz, dx) for dz in range(ZS) for dx in range(XS) if dz or dx], key=lambda p: -ring(p[0], ZS) - ring(p[1], XS)
)
SPAN_PEERS = (4, 5, 3, 2, 6, 7, 1)


def dot(lhs, rhs):
    terms = [a * b for a, b in zip(lhs, rhs)]
    while len(terms) > 1:
        terms = [terms[i] + terms[i + 1] if i + 1 < len(terms) else terms[i] for i in range(0, len(terms), 2)]
    return terms[0]


def affine(lhs, rhs, extra):
    a, b, c, d, e = [x * y for x, y in zip(lhs, rhs)]
    return ((a + b) + (c + d)) + (e + extra)


def residue(extra, lhs, rhs):
    a, b, c, d, e = [x * y for x, y in zip(lhs, rhs)]
    return (extra - e) - ((a + b) + (c + d))


def column(matrix, index):
    return [row[index] for row in matrix]


def matmul(lhs, rhs):
    cols = [column(rhs, j) for j in range(len(rhs[0]))]
    return [[dot(row, col) for col in cols] for row in lhs]


def matvec(lhs, vec):
    return [dot(row, vec) for row in lhs]


def block_transpose(tile, sub, blk):
    for d in (4, 2, 1):
        s_bit = (sub & d) != 0
        b_bit = (blk & d) != 0
        if d == 4:
            other = pltpu.roll(pltpu.roll(tile, 4, 0), 64, 1)
        else:
            up = pltpu.roll(pltpu.roll(tile, 8 - d, 0), 16 * d, 1)
            down = pltpu.roll(pltpu.roll(tile, d, 0), 128 - 16 * d, 1)
            other = jnp.where(s_bit, down, up)
        tile = jnp.where(s_bit == b_bit, tile, other)
    return tile


def skewed_transpose(tile, blk):
    tile = pltpu.roll(tile, 0, 1, stride=16, stride_axis=0)
    for d in (1, 2, 4):
        tile = jnp.where((blk & d) != 0, pltpu.roll(tile, 8 - d, 0), tile)
    return pltpu.roll(tile, 0, 1, stride=16, stride_axis=0)


def kernel(
    res_h, piv_h, low_h, upp_h, sp_h, sl_h, su_h, np_h, nl_h, nu_h,
    out_ref,
    res, low, pair, spn, sln, sun, npn, nln, nun,
    lowf, pairf, prefix, source, state, comb, send1, recv1, expand, expand2, entry, entry2, total,
    send2, recv2, unsh, carry, ysweep, wnat,
    wt, pt, lt, ut, gain, pre, alp, bet, cc, aa,
    gsend, grecv, hsend, hrecv, sentry,
    wvar, alp_v, bet_v,
    load_sem, sems,
):
    me_c = lax.axis_index("chord")
    me_s = lax.axis_index("span")

    z, x = me_c // XS, lax.rem(me_c, XS)

    def chord_peer(peer):
        return lax.rem(z + peer[0], ZS) * XS + lax.rem(x + peer[1], XS)

    barrier = pltpu.get_barrier_semaphore()
    for peer in CHORD_PEERS:
        pl.semaphore_signal(barrier, inc=1, device_id={"chord": chord_peer(peer)}, device_id_type=MESH)
    for o in SPAN_PEERS:
        pl.semaphore_signal(barrier, inc=1, device_id={"span": lax.rem(me_s + o, SPAN)}, device_id_type=MESH)

    loads = {}
    for n, src, dst in [
        (2, low_h, low), (1, piv_h, pair.at[pl.ds(0, WIDE)]), (3, upp_h, pair.at[pl.ds(WIDE, WIDE)]),
        (0, res_h, res), (4, sp_h, spn), (5, sl_h, sln),
        (6, su_h, sun), (7, np_h, npn), (8, nl_h, nln), (9, nu_h, nun),
    ]:
        copy = pltpu.make_async_copy(src, dst, load_sem.at[n])
        copy.start()
        loads[n] = copy

    sub = lax.broadcasted_iota(jnp.int32, (8, LANES), 0)
    lane = lax.broadcasted_iota(jnp.int32, (8, LANES), 1)
    blk = lane // 16

    to_row = lax.broadcasted_iota(jnp.int32, (LANES, LANES), 0)
    from_row = lax.broadcasted_iota(jnp.int32, (LANES, LANES), 1)
    order = jnp.where(from_row == HALF * lax.rem(to_row, 8) + to_row // 8, 1.0, 0.0).astype(jnp.bfloat16)

    def widen(src, dst, n):
        rows = pl.ds(pl.multiple_of(n * 128, 128), 128)
        dst[rows] = jnp.dot(order, src[rows], preferred_element_type=F32)

    def widen_low(n, _):
        widen(low, lowf, n)
        return 0

    loads[2].wait()
    lax.fori_loop(0, NV * NV, widen_low, 0, unroll=25)

    zero = jnp.zeros((8, LANES), F32)

    def tile_of(value):
        return pl.ds(8 * value, 8)

    def strided(ref, index, step):
        return ref[pl.ds(index * 128 + step, 8, stride=HALF)]

    def block(ref, index, step):
        return ref[pl.ds(pl.multiple_of(index * 128 + 8 * step, 8), 8)]

    def blocks(ref, step):
        return [[block(ref, 5 * r + c, step) for c in range(NV)] for r in range(NV)]

    def ahead_step(step):
        lows = blocks(lowf, step)
        for c in range(NV):
            new = matvec(lows, [state[tile_of(MAT + 5 * r + c)] for r in range(NV)])
            for r in range(NV):
                state[tile_of(MAT + 5 * r + c)] = new[r]
                prefix[pl.ds(pl.multiple_of((5 * r + c) * 128 + 8 * step, 8), 8)] = new[r]

    for index in range(NV * NV):
        low_0 = block(lowf, index, 0)
        state[tile_of(MAT + index)] = low_0
        prefix[pl.ds(index * 128, 8)] = low_0
    loads[1].wait()
    loads[3].wait()

    def ahead_steps(n, _):
        for t in range(3):
            ahead_step(3 * n + t + 1)
        for t in range(10):
            widen(pair, pairf, 10 * n + t)
        return 0

    lax.fori_loop(0, 5, ahead_steps, 0)
    loads[0].wait()

    def sources(step):
        cells = [strided(res, c, step) for c in range(NV)]
        src = [dot([block(pairf, 5 * r + c, step) for c in range(NV)], cells) for r in range(NV)]
        for r in range(NV):
            source[pl.ds(pl.multiple_of((step * NV + r) * 8, 8), 8)] = src[r]
        return src

    def upper(index, step):
        return block(pairf, NV * NV + index, step)

    def back_step(step, odd):
        src = sources(step)
        lows = blocks(lowf, step)
        vec = [state[tile_of(VEC + r)] for r in range(NV)]
        new = [affine(lows[r], vec, src[r]) if odd else -residue(src[r], lows[r], vec) for r in range(NV)]
        for r in range(NV):
            state[tile_of(VEC + r)] = new[r]
        mats = blocks(prefix, step)
        for r in range(NV):
            row = [state[tile_of(OUT + 5 * r + c)] for c in range(NV)]
            for c in range(NV):
                at = tile_of(INN + 5 * r + c)
                state[at] = affine(row, column(mats, c), state[at])
            at = tile_of(SRC + r)
            state[at] = affine(row, new, state[at])
        upps = [[upper(5 * r + c, step) for c in range(NV)] for r in range(NV)]
        for r in range(NV):
            row = [state[tile_of(OUT + 5 * r + c)] for c in range(NV)]
            for c in range(NV):
                state[tile_of(OUT + 5 * r + c)] = dot(row, column(upps, c))

    first = sources(0)
    for r in range(NV):
        for c in range(NV):
            state[tile_of(INN + 5 * r + c)] = block(lowf, 5 * r + c, 0)
            state[tile_of(OUT + 5 * r + c)] = upper(5 * r + c, 0)
        state[tile_of(VEC + r)] = -first[r]
        state[tile_of(SRC + r)] = -first[r]
    back_step(1, True)

    def back_pair(n, _):
        back_step(2 * n, False)
        back_step(2 * n + 1, True)
        return 0

    lax.fori_loop(1, HALF // 2, back_pair, 0)

    def half(value, which):
        return state[pl.ds(8 * value + which, NK, stride=2)]

    def half_matrix(base, which):
        return [[half(base + 5 * r + c, which) for c in range(NV)] for r in range(NV)]

    def half_vector(base, which):
        return [half(base + r, which) for r in range(NV)]

    def put(value, data):
        comb[pl.ds(NK * value, NK)] = data

    mat0 = half_matrix(MAT, 0)
    vec0 = half_vector(VEC, 0)
    mat1 = half_matrix(MAT, 1)
    mats = matmul(mat1, mat0)
    vecs = matvec(mat1, vec0)
    for r in range(NV):
        for c in range(NV):
            put(MAT + 5 * r + c, mats[r][c])
        put(VEC + r, vecs[r] + half(VEC + r, 1))
    inn1 = half_matrix(INN, 1)
    part = matmul(inn1, mat0)
    tail = [t + half(SRC + r, 1) for r, t in enumerate(matvec(inn1, vec0))]
    out0 = half_matrix(OUT, 0)
    outs = matmul(out0, half_matrix(OUT, 1))
    inns = matmul(out0, part)
    srcs = matvec(out0, tail)
    for r in range(NV):
        for c in range(NV):
            put(OUT + 5 * r + c, outs[r][c])
            put(INN + 5 * r + c, inns[r][c] + half(INN + 5 * r + c, 0))
        put(SRC + r, srcs[r] + half(SRC + r, 0))
    for value in range(85, 88):
        put(value, jnp.zeros((NK, LANES), F32))

    def shuffle(k):
        for g in range(GROUPS):
            tile = comb[pl.ds(NK * 8 * g + k, 8, stride=NK)]
            send1[pl.ds(8 * GROUPS * k + g, 8, stride=GROUPS), 0] = skewed_transpose(tile, blk)

    for k in range(NK):
        shuffle(k)

    pl.semaphore_wait(barrier, CHORD - 1 + SPAN - 1)

    def exchange(send, recv, rows, at, slot):
        for peer in CHORD_PEERS:
            to = chord_peer(peer)
            pltpu.make_async_remote_copy(
                src_ref=send.at[pl.ds(to * rows, rows)],
                dst_ref=recv.at[pl.ds(slot * rows, rows)],
                send_sem=sems.at[2 * at],
                recv_sem=sems.at[2 * at + 1],
                device_id={"chord": to},
                device_id_type=MESH,
            ).start()
        recv[pl.ds(slot * rows, rows)] = send[pl.ds(me_c * rows, rows)]

    def spread(send, recv, rows, at):
        for o in SPAN_PEERS:
            pltpu.make_async_remote_copy(
                src_ref=send,
                dst_ref=recv.at[pl.ds(me_s * rows, rows)],
                send_sem=sems.at[2 * at],
                recv_sem=sems.at[2 * at + 1],
                device_id={"span": lax.rem(me_s + o, SPAN)},
                device_id_type=MESH,
            ).start()
        recv[pl.ds(me_s * rows, rows)] = send[...]

    def settle(ref, rows, sem):
        whole = ref.at[pl.ds(0, rows)]
        pltpu.make_async_copy(whole, whole, sems.at[sem]).wait()

    exchange(send1, recv1, GROUPS, 0, me_c)

    for n, (src, dst) in enumerate([(spn, pt), (sln, lt), (sun, ut)]):
        loads[4 + n].wait()
        for v in range(NV):
            dst[pl.ds(v, LANES, stride=8)] = src[pl.ds(128 * v, 128)].T

    def at_j(j):
        return pl.ds(pl.multiple_of(8 * j, 8), NV)

    ones5 = jnp.ones((NV, LANES), F32)
    zeros5 = jnp.zeros((NV, LANES), F32)

    def gains_ahead(j, held):
        g, p = held
        g = -(lt[at_j(j)] * g)
        gain[at_j(j)] = g
        pre[at_j(j)] = p
        return (g, -(ut[at_j(j)] * p))

    g_end, _ = lax.fori_loop(0, LANES, gains_ahead, (ones5, ones5), unroll=8)

    def gains_back(n, held):
        suf, b, c, a, low_next = held
        j = LANES - 1 - n
        l, u, p = lt[at_j(j)], ut[at_j(j)], pt[at_j(j)]
        alp[at_j(j)] = suf * p
        b = pre[at_j(j)] - low_next * b
        bet[at_j(j)] = b * p
        c = -(u * c)
        cc[at_j(j)] = c
        a = gain[at_j(j)] - u * a
        aa[at_j(j)] = a
        return (-(l * suf), b, c, a, l)

    _, _, c_top, a_top, _ = lax.fori_loop(
        0, LANES, gains_back, (ones5, zeros5, ones5, zeros5, zeros5), unroll=8
    )
    gsend[pl.ds(0, NV), 0] = g_end
    gsend[pl.ds(NV, NV), 0] = a_top
    gsend[pl.ds(2 * NV, NV), 0] = c_top
    spread(gsend, grecv, 3 * NV, 2)
    for v in range(NV):
        alp_v[pl.ds(128 * v, 128)] = alp[pl.ds(v, LANES, stride=8)]
        bet_v[pl.ds(128 * v, 128)] = bet[pl.ds(v, LANES, stride=8)]

    settle(recv1, (CHORD - 1) * GROUPS, 1)

    ahead_values = 8 * (OUT // 8 + 1)

    def unpack(q, groups):
        for g in groups:
            tile = recv1[pl.ds(8 * GROUPS * q + g, 8, stride=GROUPS), 0]
            for s in range(8):
                value = 8 * g + s
                if value < 85:
                    moved = tile if s == 0 else pltpu.roll(tile, LANES - 16 * s, 1)
                    if value < ahead_values:
                        expand[pl.ds(pl.multiple_of(CHORD * value + 8 * q, 8), 8)] = moved
                    if value >= OUT:
                        expand2[pl.ds(pl.multiple_of(CHORD * (value - OUT) + 8 * q, 8), 8)] = moved

    def row(value, at):
        return expand[pl.ds(CHORD * value + at, 1)]

    def row2(value, at):
        return expand2[pl.ds(CHORD * (value - OUT) + at, 1)]

    def tile2(value, q):
        return expand2[pl.ds(pl.multiple_of(CHORD * (value - OUT) + 8 * q, 8), 8)]

    def relay_ahead(q, held):
        for n in range(8):
            at = 8 * q + n
            new = []
            for c in range(NV):
                entry[pl.ds(CHORD * c + at, 1)] = held[c]
            for r in range(NV):
                new.append(affine([row(MAT + 5 * r + c, at) for c in range(NV)], held, row(VEC + r, at)))
            held = new
        return held

    held = [jnp.zeros((1, LANES), F32) for _ in range(NV)]
    for q in range(CHORD // 8):
        unpack(q, range(ahead_values // 8))
    for q in range(CHORD // 8):
        held = relay_ahead(q, held)
        unpack(q, range(ahead_values // 8, GROUPS))

    for q in range(CHORD // 8):
        vec = [entry[pl.ds(CHORD * c + 8 * q, 8)] for c in range(NV)]
        for r in range(NV):
            mats_r = [tile2(INN + 5 * r + c, q) for c in range(NV)]
            total[pl.ds(CHORD * r + 8 * q, 8)] = -affine(mats_r, vec, tile2(SRC + r, q))

    def relay_back(q, held):
        for n in reversed(range(8)):
            at = 8 * q + n
            new = []
            for c in range(NV):
                entry2[pl.ds(CHORD * c + at, 1)] = held[c]
            for r in range(NV):
                new.append(
                    affine([row2(OUT + 5 * r + c, at) for c in range(NV)], held, total[pl.ds(CHORD * r + at, 1)])
                )
            held = new
        return held

    held = [jnp.zeros((1, LANES), F32) for _ in range(NV)]
    for q in reversed(range(CHORD // 8)):
        held = relay_back(q, held)

    for q in range(CHORD // 8):
        for kind in range(2):
            tile = zero
            for s in range(NV):
                part_s = (entry2 if kind else entry)[pl.ds(CHORD * s + 8 * q, 8)]
                if s > 0:
                    part_s = pltpu.roll(part_s, 16 * s, 1)
                tile = jnp.where(blk == s, part_s, tile)
            send2[pl.ds(16 * q + kind, 8, stride=2), 0] = tile

    exchange(send2, recv2, 2, 1, me_c // 8 * 8 + lax.rem(8 - lax.rem(me_c, 8), 8))

    settle(recv2, (CHORD - 1) * 2, 3)

    for kind in range(2):
        for k in range(NK):
            tile = recv2[pl.ds(16 * k + kind, 8, stride=2), 0]
            unsh[pl.ds(8 * (NK * kind + k), 8)] = block_transpose(tile, sub, blk)
    a0 = [unsh[pl.ds(v, NK, stride=8)] for v in range(NV)]
    c1 = [unsh[pl.ds(8 * NK + v, NK, stride=8)] for v in range(NV)]
    a1 = [m + half(VEC + r, 0) for r, m in enumerate(matvec(half_matrix(MAT, 0), a0))]
    back = matvec(half_matrix(OUT, 1), c1)
    fore = matvec(half_matrix(INN, 1), a1)
    c0 = [back[r] - (fore[r] + half(SRC + r, 1)) for r in range(NV)]
    for v in range(NV):
        carry[pl.ds(8 * v, NK, stride=2)] = a0[v]
        carry[pl.ds(8 * v + 1, NK, stride=2)] = a1[v]
        carry[pl.ds(8 * (NV + v), NK, stride=2)] = c0[v]
        carry[pl.ds(8 * (NV + v) + 1, NK, stride=2)] = c1[v]

    def by_step(ref, step, r):
        return [block(ref, NV * r + c, step) for c in range(NV)]

    def sweep_ahead(step, held):
        new = []
        for r in range(NV):
            at = pl.ds(pl.multiple_of((step * NV + r) * 8, 8), 8)
            val = residue(source[at], by_step(lowf, step, r), held)
            ysweep[at] = val
            new.append(val)
        return tuple(new)

    lax.fori_loop(0, HALF, sweep_ahead, tuple(carry[tile_of(v)] for v in range(NV)), unroll=16)

    def sweep_back(n, held):
        step = HALF - 1 - n
        new = []
        for r in range(NV):
            at = pl.ds(pl.multiple_of((step * NV + r) * 8, 8), 8)
            val = residue(ysweep[at], by_step(pairf, step, r + NV), held)
            wnat[pl.ds(128 * r + step, 8, stride=HALF)] = val
            new.append(val)
        return tuple(new)

    lax.fori_loop(0, HALF, sweep_back, tuple(carry[tile_of(NV + v)] for v in range(NV)), unroll=16)

    for v in range(NV):
        turned = wnat[pl.ds(128 * v, 128)].T
        wvar[pl.ds(128 * v, 128)] = turned
        for kind, weight in enumerate((alp_v, bet_v)):
            terms = [turned[8 * t : 8 * t + 8] * weight[pl.ds(128 * v + 8 * t, 8)] for t in range(16)]
            while len(terms) > 1:
                terms = [terms[t] + terms[t + 1] for t in range(0, len(terms), 2)]
            hsend[pl.ds(NV * kind + v, 1), 0] = jnp.sum(terms[0], axis=0, keepdims=True)
    spread(hsend, hrecv, 2 * NV, 3)
    for v in range(NV):
        wt[pl.ds(v, LANES, stride=8)] = wvar[pl.ds(128 * v, 128)]

    def span_ahead(j, z):
        z = pt[at_j(j)] * wt[at_j(j)] - lt[at_j(j)] * z
        wt[at_j(j)] = z
        return z

    lax.fori_loop(0, LANES, span_ahead, zeros5, unroll=8)

    def span_back(n, z):
        j = LANES - 1 - n
        z = wt[at_j(j)] - ut[at_j(j)] * z
        wt[at_j(j)] = z
        return z

    lax.fori_loop(0, LANES, span_back, zeros5, unroll=8)

    settle(grecv, (SPAN - 1) * 3 * NV, 5)
    settle(hrecv, (SPAN - 1) * 2 * NV, 7)
    a = zeros5
    sent = []
    for d in range(SPAN):
        sentry[pl.ds(8 * d, NV)] = a
        sent.append(a)
        a = hrecv[pl.ds(2 * NV * d, NV), 0] + grecv[pl.ds(3 * NV * d, NV), 0] * a
    c = zeros5
    for d in reversed(range(SPAN)):
        sentry[pl.ds(8 * (SPAN + d), NV)] = c
        c = (
            hrecv[pl.ds(2 * NV * d + NV, NV), 0]
            + grecv[pl.ds(3 * NV * d + NV, NV), 0] * sent[d]
            + grecv[pl.ds(3 * NV * d + 2 * NV, NV), 0] * c
        )
    a_in = sentry[pl.ds(pl.multiple_of(8 * me_s, 8), NV)]
    c_in = sentry[pl.ds(pl.multiple_of(8 * (SPAN + me_s), 8), NV)]

    def close(j, _):
        wt[at_j(j)] = wt[at_j(j)] + aa[at_j(j)] * a_in + cc[at_j(j)] * c_in
        return 0

    lax.fori_loop(0, LANES, close, 0, unroll=32)

    for n in range(7, 10):
        loads[n].wait()
    for v in range(NV):
        x = wt[pl.ds(v, LANES, stride=8)].T
        held = None
        planes = []
        for k in range(NK):
            at = pl.ds(128 * v + 32 * k, 32)
            now = npn[at].astype(F32) * x[32 * k : 32 * k + 32]
            held = now if held is None else now - nln[at].astype(F32) * held
            planes.append(held)
        held = None
        for k in reversed(range(NK)):
            at = pl.ds(128 * v + 32 * k, 32)
            held = planes[k] if held is None else planes[k] - nun[at].astype(F32) * held
            out_ref[at] = held

    settle(send1, (CHORD - 1) * GROUPS, 0)
    settle(send2, (CHORD - 1) * 2, 2)
    settle(grecv, (SPAN - 1) * 3 * NV, 4)
    settle(hrecv, (SPAN - 1) * 2 * NV, 6)


def on_device(*args):
    flat = [a.reshape(-1, LANES) for a in args]
    f32 = lambda *shape: pltpu.VMEM(shape, F32)
    b16 = lambda *shape: pltpu.VMEM(shape, jnp.bfloat16)
    wide, narrow = NV * NV * 128, NV * 128
    scratch = [
        f32(narrow, LANES), b16(wide, LANES), b16(2 * wide, LANES),
        f32(narrow, LANES), f32(narrow, LANES), f32(narrow, LANES),
        b16(narrow, LANES), b16(narrow, LANES), b16(narrow, LANES),
        f32(wide, LANES), f32(2 * wide, LANES), f32(wide, LANES),
        f32(HALF * NV * 8, LANES),
        f32(88 * 8, LANES),
        f32(88 * NK, LANES),
        f32(CHORD * GROUPS, 1, LANES), f32(CHORD * GROUPS, 1, LANES),
        f32(32 * CHORD, LANES), f32(55 * CHORD, LANES),
        f32(NV * CHORD, LANES), f32(NV * CHORD, LANES), f32(NV * CHORD, LANES),
        f32(2 * CHORD, 1, LANES), f32(2 * CHORD, 1, LANES),
        f32(64, LANES), f32(80, LANES),
        f32(HALF * NV * 8, LANES), f32(narrow, LANES),
    ]
    scratch += [f32(8 * LANES, LANES) for _ in range(10)]
    scratch += [
        f32(3 * NV, 1, LANES), f32(SPAN * 3 * NV, 1, LANES),
        f32(2 * NV, 1, LANES), f32(SPAN * 2 * NV, 1, LANES),
        f32(2 * SPAN * 8, LANES),
        f32(narrow, LANES), f32(narrow, LANES), f32(narrow, LANES),
        pltpu.SemaphoreType.DMA((10,)),
        pltpu.SemaphoreType.DMA((8,)),
    ]
    out = pl.pallas_call(
        kernel,
        out_shape=pltpu.VMEM((narrow, LANES), F32),
        in_specs=[pl.BlockSpec(memory_space=pl.ANY)] * 10,
        out_specs=pl.BlockSpec(memory_space=pltpu.VMEM),
        scratch_shapes=scratch,
        compiler_params=pltpu.CompilerParams(
            collective_id=0, has_side_effects=True, vmem_limit_bytes=60 * 1024 * 1024
        ),
    )(*flat)
    return out.reshape(NV, NK, CELLS, LANES)


def solution(mesh):
    grid = P(None, None, "chord", "span")
    deep = P(None, None, None, "chord", "span")
    return jax.shard_map(
        on_device,
        mesh=mesh,
        in_specs=(grid, deep, deep, deep, grid, grid, grid, grid, grid, grid),
        out_specs=grid,
        check_vma=False,
    )
```

```python
import functools

import jax
import jax.numpy as jnp
from jax import lax
from jax.experimental import pallas as pl
from jax.experimental.pallas import tpu as pltpu
from jax.sharding import PartitionSpec as P

F32 = jnp.float32
MESH = pl.DeviceIdType.MESH

NV = 5
NK = 4
CHORD = 32
SPAN = 8
CELLS = 32
LANES = 128
HALF = 16
GROUPS = 11
MAT, VEC, OUT, INN, SRC = 0, 25, 30, 55, 80
ZS, XS = 8, 4
WIDE = NV * NV * 128


def ring(step, size):
    return min(step, size - step)


CHORD_PEERS = sorted(
    [(dz, dx) for dz in range(ZS) for dx in range(XS) if dz or dx], key=lambda p: -ring(p[0], ZS) - ring(p[1], XS)
)
SPAN_PEERS = (4, 5, 3, 2, 6, 7, 1)


def dot(lhs, rhs):
    terms = [a * b for a, b in zip(lhs, rhs)]
    while len(terms) > 1:
        terms = [terms[i] + terms[i + 1] if i + 1 < len(terms) else terms[i] for i in range(0, len(terms), 2)]
    return terms[0]


def affine(lhs, rhs, extra):
    a, b, c, d, e = [x * y for x, y in zip(lhs, rhs)]
    return ((a + b) + (c + d)) + (e + extra)


def residue(extra, lhs, rhs):
    a, b, c, d, e = [x * y for x, y in zip(lhs, rhs)]
    return (extra - e) - ((a + b) + (c + d))


def column(matrix, index):
    return [row[index] for row in matrix]


def matmul(lhs, rhs):
    cols = [column(rhs, j) for j in range(len(rhs[0]))]
    return [[dot(row, col) for col in cols] for row in lhs]


def matvec(lhs, vec):
    return [dot(row, vec) for row in lhs]


def skewed_transpose(tile, blk):
    tile = pltpu.roll(tile, 0, 1, stride=16, stride_axis=0)
    for d in (1, 2, 4):
        tile = jnp.where((blk & d) != 0, pltpu.roll(tile, 8 - d, 0), tile)
    return pltpu.roll(tile, 0, 1, stride=16, stride_axis=0)


def kernel(
    res_h, piv_h, low_h, upp_h, sp_h, sl_h, su_h, np_h, nl_h, nu_h,
    out_ref,
    res, low, pair, spn, sln, sun, npn, nln, nun,
    lowf, pairf, prefix, source, state, comb, send1, recv1, expand, expand2, entry, entry2, total,
    send2, recv2, unsh, carry, ysweep, wnat,
    wt, pt, lt, ut, gain, pre, alp, bet, cc, aa,
    gsend, grecv, hsend, hrecv, sentry,
    wvar, alp_v, bet_v,
    load_sem, sems,
):
    me_c = lax.axis_index("chord")
    me_s = lax.axis_index("span")

    z, x = me_c // XS, lax.rem(me_c, XS)

    def chord_peer(peer):
        return lax.rem(z + peer[0], ZS) * XS + lax.rem(x + peer[1], XS)

    barrier = pltpu.get_barrier_semaphore()
    for peer in CHORD_PEERS:
        pl.semaphore_signal(barrier, inc=1, device_id={"chord": chord_peer(peer)}, device_id_type=MESH)
    for o in SPAN_PEERS:
        pl.semaphore_signal(barrier, inc=1, device_id={"span": lax.rem(me_s + o, SPAN)}, device_id_type=MESH)

    loads = {}
    for n, src, dst in [
        (2, low_h, low), (1, piv_h, pair.at[pl.ds(0, WIDE)]), (3, upp_h, pair.at[pl.ds(WIDE, WIDE)]),
        (0, res_h, res), (4, sp_h, spn), (5, sl_h, sln),
        (6, su_h, sun), (7, np_h, npn), (8, nl_h, nln), (9, nu_h, nun),
    ]:
        copy = pltpu.make_async_copy(src, dst, load_sem.at[n])
        copy.start()
        loads[n] = copy

    lane = lax.broadcasted_iota(jnp.int32, (8, LANES), 1)
    blk = lane // 16

    to_row = lax.broadcasted_iota(jnp.int32, (LANES, LANES), 0)
    from_row = lax.broadcasted_iota(jnp.int32, (LANES, LANES), 1)
    order = jnp.where(from_row == HALF * lax.rem(to_row, 8) + to_row // 8, 1.0, 0.0).astype(jnp.bfloat16)

    def widen(src, dst, n):
        rows = pl.ds(pl.multiple_of(n * 128, 128), 128)
        dst[rows] = jnp.dot(order, src[rows], preferred_element_type=F32)

    loads[2].wait()
    for n in range(NV):
        rows = [pl.ds(128 * (NV * n + c), 128) for c in range(NV)]
        abreast = jnp.dot(order, jnp.concatenate([low[at] for at in rows], axis=1), preferred_element_type=F32)
        for c in range(NV):
            lowf[rows[c]] = abreast[:, 128 * c : 128 * c + 128]

    zero = jnp.zeros((8, LANES), F32)

    def tile_of(value):
        return pl.ds(8 * value, 8)

    def strided(ref, index, step):
        return ref[pl.ds(index * 128 + step, 8, stride=HALF)]

    def block(ref, index, step):
        return ref[pl.ds(pl.multiple_of(index * 128 + 8 * step, 8), 8)]

    def blocks(ref, step):
        return [[block(ref, 5 * r + c, step) for c in range(NV)] for r in range(NV)]

    def ahead_step(step):
        lows = blocks(lowf, step)
        for c in range(NV):
            new = matvec(lows, [state[tile_of(MAT + 5 * r + c)] for r in range(NV)])
            for r in range(NV):
                state[tile_of(MAT + 5 * r + c)] = new[r]
                prefix[pl.ds(pl.multiple_of((5 * r + c) * 128 + 8 * step, 8), 8)] = new[r]

    for index in range(NV * NV):
        low_0 = block(lowf, index, 0)
        state[tile_of(MAT + index)] = low_0
        prefix[pl.ds(index * 128, 8)] = low_0
    loads[1].wait()
    loads[3].wait()

    def ahead_steps(n, _):
        for t in range(3):
            ahead_step(3 * n + t + 1)
        for t in range(10):
            widen(pair, pairf, 10 * n + t)
        return 0

    lax.fori_loop(0, 5, ahead_steps, 0)
    loads[0].wait()

    def sources(step):
        cells = [strided(res, c, step) for c in range(NV)]
        src = [dot([block(pairf, 5 * r + c, step) for c in range(NV)], cells) for r in range(NV)]
        for r in range(NV):
            source[pl.ds(pl.multiple_of((step * NV + r) * 8, 8), 8)] = src[r]
        return src

    def upper(index, step):
        return block(pairf, NV * NV + index, step)

    def back_step(step, odd):
        src = sources(step)
        lows = blocks(lowf, step)
        vec = [state[tile_of(VEC + r)] for r in range(NV)]
        new = [affine(lows[r], vec, src[r]) if odd else -residue(src[r], lows[r], vec) for r in range(NV)]
        for r in range(NV):
            state[tile_of(VEC + r)] = new[r]
        mats = blocks(prefix, step)
        for r in range(NV):
            row = [state[tile_of(OUT + 5 * r + c)] for c in range(NV)]
            for c in range(NV):
                at = tile_of(INN + 5 * r + c)
                state[at] = affine(row, column(mats, c), state[at])
            at = tile_of(SRC + r)
            state[at] = affine(row, new, state[at])
        upps = [[upper(5 * r + c, step) for c in range(NV)] for r in range(NV)]
        for r in range(NV):
            row = [state[tile_of(OUT + 5 * r + c)] for c in range(NV)]
            for c in range(NV):
                state[tile_of(OUT + 5 * r + c)] = dot(row, column(upps, c))

    first = sources(0)
    for r in range(NV):
        for c in range(NV):
            state[tile_of(INN + 5 * r + c)] = block(lowf, 5 * r + c, 0)
            state[tile_of(OUT + 5 * r + c)] = upper(5 * r + c, 0)
        state[tile_of(VEC + r)] = -first[r]
        state[tile_of(SRC + r)] = -first[r]
    back_step(1, True)

    def back_pair(n, _):
        back_step(2 * n, False)
        back_step(2 * n + 1, True)
        return 0

    lax.fori_loop(1, HALF // 2, back_pair, 0)

    def half(value, which):
        return state[pl.ds(8 * value + which, NK, stride=2)]

    def half_matrix(base, which):
        return [[half(base + 5 * r + c, which) for c in range(NV)] for r in range(NV)]

    def half_vector(base, which):
        return [half(base + r, which) for r in range(NV)]

    def put(value, data):
        comb[pl.ds(NK * value, NK)] = data

    mat0 = half_matrix(MAT, 0)
    vec0 = half_vector(VEC, 0)
    mat1 = half_matrix(MAT, 1)
    mats = matmul(mat1, mat0)
    vecs = matvec(mat1, vec0)
    for r in range(NV):
        for c in range(NV):
            put(MAT + 5 * r + c, mats[r][c])
        put(VEC + r, vecs[r] + half(VEC + r, 1))
    inn1 = half_matrix(INN, 1)
    part = matmul(inn1, mat0)
    tail = [t + half(SRC + r, 1) for r, t in enumerate(matvec(inn1, vec0))]
    out0 = half_matrix(OUT, 0)
    outs = matmul(out0, half_matrix(OUT, 1))
    inns = matmul(out0, part)
    srcs = matvec(out0, tail)
    for r in range(NV):
        for c in range(NV):
            put(OUT + 5 * r + c, outs[r][c])
            put(INN + 5 * r + c, inns[r][c] + half(INN + 5 * r + c, 0))
        put(SRC + r, srcs[r] + half(SRC + r, 0))
    for value in range(85, 88):
        put(value, jnp.zeros((NK, LANES), F32))

    def shuffle(k):
        for g in range(GROUPS):
            tile = comb[pl.ds(NK * 8 * g + k, 8, stride=NK)]
            send1[pl.ds(8 * GROUPS * k + g, 8, stride=GROUPS), 0] = skewed_transpose(tile, blk)

    for k in range(NK):
        shuffle(k)

    pl.semaphore_wait(barrier, CHORD - 1 + SPAN - 1)

    def exchange(send, recv, rows, at, slot):
        for peer in CHORD_PEERS:
            to = chord_peer(peer)
            pltpu.make_async_remote_copy(
                src_ref=send.at[pl.ds(to * rows, rows)],
                dst_ref=recv.at[pl.ds(slot * rows, rows)],
                send_sem=sems.at[2 * at],
                recv_sem=sems.at[2 * at + 1],
                device_id={"chord": to},
                device_id_type=MESH,
            ).start()
        recv[pl.ds(slot * rows, rows)] = send[pl.ds(me_c * rows, rows)]

    def spread(send, recv, rows, at):
        for o in SPAN_PEERS:
            pltpu.make_async_remote_copy(
                src_ref=send,
                dst_ref=recv.at[pl.ds(me_s * rows, rows)],
                send_sem=sems.at[2 * at],
                recv_sem=sems.at[2 * at + 1],
                device_id={"span": lax.rem(me_s + o, SPAN)},
                device_id_type=MESH,
            ).start()
        recv[pl.ds(me_s * rows, rows)] = send[...]

    def settle(ref, rows, sem):
        whole = ref.at[pl.ds(0, rows)]
        pltpu.make_async_copy(whole, whole, sems.at[sem]).wait()

    exchange(send1, recv1, GROUPS, 0, me_c)

    for n, (src, dst) in enumerate([(spn, pt), (sln, lt), (sun, ut)]):
        loads[4 + n].wait()
        for v in range(NV):
            dst[pl.ds(v, LANES, stride=8)] = src[pl.ds(128 * v, 128)].T

    def at_j(j):
        return pl.ds(pl.multiple_of(8 * j, 8), NV)

    ones5 = jnp.ones((NV, LANES), F32)
    zeros5 = jnp.zeros((NV, LANES), F32)

    def gains_ahead(j, held):
        g, p = held
        g = -(lt[at_j(j)] * g)
        gain[at_j(j)] = g
        pre[at_j(j)] = p
        return (g, -(ut[at_j(j)] * p))

    g_end, _ = lax.fori_loop(0, LANES, gains_ahead, (ones5, ones5), unroll=8)

    def gains_back(n, held):
        suf, b, c, a, low_next = held
        j = LANES - 1 - n
        l, u, p = lt[at_j(j)], ut[at_j(j)], pt[at_j(j)]
        alp[at_j(j)] = suf * p
        b = pre[at_j(j)] - low_next * b
        bet[at_j(j)] = b * p
        c = -(u * c)
        cc[at_j(j)] = c
        a = gain[at_j(j)] - u * a
        aa[at_j(j)] = a
        return (-(l * suf), b, c, a, l)

    _, _, c_top, a_top, _ = lax.fori_loop(
        0, LANES, gains_back, (ones5, zeros5, ones5, zeros5, zeros5), unroll=8
    )
    gsend[pl.ds(0, NV), 0] = g_end
    gsend[pl.ds(NV, NV), 0] = a_top
    gsend[pl.ds(2 * NV, NV), 0] = c_top
    spread(gsend, grecv, 3 * NV, 2)
    for v in range(NV):
        alp_v[pl.ds(128 * v, 128)] = alp[pl.ds(v, LANES, stride=8)]
        bet_v[pl.ds(128 * v, 128)] = bet[pl.ds(v, LANES, stride=8)]

    settle(recv1, (CHORD - 1) * GROUPS, 1)

    ahead_values = 8 * (OUT // 8 + 1)

    def unpack(q, groups):
        for g in groups:
            tile = recv1[pl.ds(8 * GROUPS * q + g, 8, stride=GROUPS), 0]
            for s in range(8):
                value = 8 * g + s
                if value < 85:
                    moved = tile if s == 0 else pltpu.roll(tile, LANES - 16 * s, 1)
                    if value < ahead_values:
                        expand[pl.ds(pl.multiple_of(CHORD * value + 8 * q, 8), 8)] = moved
                    if value >= OUT:
                        expand2[pl.ds(pl.multiple_of(CHORD * (value - OUT) + 8 * q, 8), 8)] = moved

    def row(value, at):
        return expand[pl.ds(CHORD * value + at, 1)]

    def row2(value, at):
        return expand2[pl.ds(CHORD * (value - OUT) + at, 1)]

    def tile2(value, q):
        return expand2[pl.ds(pl.multiple_of(CHORD * (value - OUT) + 8 * q, 8), 8)]

    def relay_ahead(q, held):
        for n in range(8):
            at = 8 * q + n
            new = []
            for c in range(NV):
                entry[pl.ds(CHORD * c + at, 1)] = held[c]
            for r in range(NV):
                new.append(affine([row(MAT + 5 * r + c, at) for c in range(NV)], held, row(VEC + r, at)))
            held = new
        return held

    held = [jnp.zeros((1, LANES), F32) for _ in range(NV)]
    for q in range(CHORD // 8):
        unpack(q, range(ahead_values // 8))
    for q in range(CHORD // 8):
        held = relay_ahead(q, held)
        unpack(q, range(ahead_values // 8, GROUPS))

    for q in range(CHORD // 8):
        vec = [entry[pl.ds(CHORD * c + 8 * q, 8)] for c in range(NV)]
        for r in range(NV):
            mats_r = [tile2(INN + 5 * r + c, q) for c in range(NV)]
            total[pl.ds(CHORD * r + 8 * q, 8)] = -affine(mats_r, vec, tile2(SRC + r, q))

    def relay_back(q, held):
        for n in reversed(range(8)):
            at = 8 * q + n
            new = []
            for c in range(NV):
                entry2[pl.ds(CHORD * c + at, 1)] = held[c]
            for r in range(NV):
                new.append(
                    affine([row2(OUT + 5 * r + c, at) for c in range(NV)], held, total[pl.ds(CHORD * r + at, 1)])
                )
            held = new
        return held

    held = [jnp.zeros((1, LANES), F32) for _ in range(NV)]
    for q in reversed(range(CHORD // 8)):
        held = relay_back(q, held)

    for q in range(CHORD // 8):
        for kind in range(2):
            tile = zero
            for s in range(NV):
                part_s = (entry2 if kind else entry)[pl.ds(CHORD * s + 8 * q, 8)]
                if s > 0:
                    part_s = pltpu.roll(part_s, 16 * s, 1)
                tile = jnp.where(blk == s, part_s, tile)
            send2[pl.ds(16 * q + kind, 8, stride=2), 0] = tile

    exchange(send2, recv2, 2, 1, me_c // 8 * 8 + lax.rem(8 - lax.rem(me_c, 8), 8))

    settle(recv2, (CHORD - 1) * 2, 3)

    for kind in range(2):
        for k in range(NK):
            tile = recv2[pl.ds(16 * k + kind, 8, stride=2), 0]
            unsh[pl.ds(8 * (NK * kind + k), 8)] = skewed_transpose(tile, blk)
    a0 = [unsh[pl.ds((8 - v) % 8, NK, stride=8)] for v in range(NV)]
    c1 = [unsh[pl.ds(8 * NK + (8 - v) % 8, NK, stride=8)] for v in range(NV)]
    a1 = [m + half(VEC + r, 0) for r, m in enumerate(matvec(half_matrix(MAT, 0), a0))]
    back = matvec(half_matrix(OUT, 1), c1)
    fore = matvec(half_matrix(INN, 1), a1)
    c0 = [back[r] - (fore[r] + half(SRC + r, 1)) for r in range(NV)]
    for v in range(NV):
        carry[pl.ds(8 * v, NK, stride=2)] = a0[v]
        carry[pl.ds(8 * v + 1, NK, stride=2)] = a1[v]
        carry[pl.ds(8 * (NV + v), NK, stride=2)] = c0[v]
        carry[pl.ds(8 * (NV + v) + 1, NK, stride=2)] = c1[v]

    def by_step(ref, step, r):
        return [block(ref, NV * r + c, step) for c in range(NV)]

    def sweep_ahead(step, held):
        new = []
        for r in range(NV):
            at = pl.ds(pl.multiple_of((step * NV + r) * 8, 8), 8)
            val = residue(source[at], by_step(lowf, step, r), held)
            ysweep[at] = val
            new.append(val)
        return tuple(new)

    lax.fori_loop(0, HALF, sweep_ahead, tuple(carry[tile_of(v)] for v in range(NV)), unroll=16)

    def sweep_back(n, held):
        step = HALF - 1 - n
        new = []
        for r in range(NV):
            at = pl.ds(pl.multiple_of((step * NV + r) * 8, 8), 8)
            val = residue(ysweep[at], by_step(pairf, step, r + NV), held)
            wnat[pl.ds(128 * r + step, 8, stride=HALF)] = val
            new.append(val)
        return tuple(new)

    lax.fori_loop(0, HALF, sweep_back, tuple(carry[tile_of(NV + v)] for v in range(NV)), unroll=16)

    for v in range(NV):
        turned = wnat[pl.ds(128 * v, 128)].T
        wvar[pl.ds(128 * v, 128)] = turned
        for kind, weight in enumerate((alp_v, bet_v)):
            terms = [turned[8 * t : 8 * t + 8] * weight[pl.ds(128 * v + 8 * t, 8)] for t in range(16)]
            while len(terms) > 1:
                terms = [terms[t] + terms[t + 1] for t in range(0, len(terms), 2)]
            hsend[pl.ds(NV * kind + v, 1), 0] = jnp.sum(terms[0], axis=0, keepdims=True)
    spread(hsend, hrecv, 2 * NV, 3)
    for v in range(NV):
        wt[pl.ds(v, LANES, stride=8)] = wvar[pl.ds(128 * v, 128)]

    def span_ahead(j, z):
        z = pt[at_j(j)] * wt[at_j(j)] - lt[at_j(j)] * z
        wt[at_j(j)] = z
        return z

    lax.fori_loop(0, LANES, span_ahead, zeros5, unroll=8)

    def span_back(n, z):
        j = LANES - 1 - n
        z = wt[at_j(j)] - ut[at_j(j)] * z
        wt[at_j(j)] = z
        return z

    lax.fori_loop(0, LANES, span_back, zeros5, unroll=8)

    settle(grecv, (SPAN - 1) * 3 * NV, 5)
    settle(hrecv, (SPAN - 1) * 2 * NV, 7)
    a = zeros5
    sent = []
    for d in range(SPAN):
        sentry[pl.ds(8 * d, NV)] = a
        sent.append(a)
        a = hrecv[pl.ds(2 * NV * d, NV), 0] + grecv[pl.ds(3 * NV * d, NV), 0] * a
    c = zeros5
    for d in reversed(range(SPAN)):
        sentry[pl.ds(8 * (SPAN + d), NV)] = c
        c = (
            hrecv[pl.ds(2 * NV * d + NV, NV), 0]
            + grecv[pl.ds(3 * NV * d + NV, NV), 0] * sent[d]
            + grecv[pl.ds(3 * NV * d + 2 * NV, NV), 0] * c
        )
    a_in = sentry[pl.ds(pl.multiple_of(8 * me_s, 8), NV)]
    c_in = sentry[pl.ds(pl.multiple_of(8 * (SPAN + me_s), 8), NV)]

    def close(j, _):
        wt[at_j(j)] = wt[at_j(j)] + aa[at_j(j)] * a_in + cc[at_j(j)] * c_in
        return 0

    lax.fori_loop(0, LANES, close, 0, unroll=32)

    for n in range(7, 10):
        loads[n].wait()
    for v in range(NV):
        x = wt[pl.ds(v, LANES, stride=8)].T
        held = None
        planes = []
        for k in range(NK):
            at = pl.ds(128 * v + 32 * k, 32)
            now = npn[at].astype(F32) * x[32 * k : 32 * k + 32]
            held = now if held is None else now - nln[at].astype(F32) * held
            planes.append(held)
        held = None
        for k in reversed(range(NK)):
            at = pl.ds(128 * v + 32 * k, 32)
            held = planes[k] if held is None else planes[k] - nun[at].astype(F32) * held
            out_ref[at] = held

    settle(send1, (CHORD - 1) * GROUPS, 0)
    settle(send2, (CHORD - 1) * 2, 2)
    settle(grecv, (SPAN - 1) * 3 * NV, 4)
    settle(hrecv, (SPAN - 1) * 2 * NV, 6)


def on_device(*args):
    flat = [a.reshape(-1, LANES) for a in args]
    f32 = lambda *shape: pltpu.VMEM(shape, F32)
    b16 = lambda *shape: pltpu.VMEM(shape, jnp.bfloat16)
    wide, narrow = NV * NV * 128, NV * 128
    scratch = [
        f32(narrow, LANES), b16(wide, LANES), b16(2 * wide, LANES),
        f32(narrow, LANES), f32(narrow, LANES), f32(narrow, LANES),
        b16(narrow, LANES), b16(narrow, LANES), b16(narrow, LANES),
        f32(wide, LANES), f32(2 * wide, LANES), f32(wide, LANES),
        f32(HALF * NV * 8, LANES),
        f32(88 * 8, LANES),
        f32(88 * NK, LANES),
        f32(CHORD * GROUPS, 1, LANES), f32(CHORD * GROUPS, 1, LANES),
        f32(32 * CHORD, LANES), f32(55 * CHORD, LANES),
        f32(NV * CHORD, LANES), f32(NV * CHORD, LANES), f32(NV * CHORD, LANES),
        f32(2 * CHORD, 1, LANES), f32(2 * CHORD, 1, LANES),
        f32(64, LANES), f32(80, LANES),
        f32(HALF * NV * 8, LANES), f32(narrow, LANES),
    ]
    scratch += [f32(8 * LANES, LANES) for _ in range(10)]
    scratch += [
        f32(3 * NV, 1, LANES), f32(SPAN * 3 * NV, 1, LANES),
        f32(2 * NV, 1, LANES), f32(SPAN * 2 * NV, 1, LANES),
        f32(2 * SPAN * 8, LANES),
        f32(narrow, LANES), f32(narrow, LANES), f32(narrow, LANES),
        pltpu.SemaphoreType.DMA((10,)),
        pltpu.SemaphoreType.DMA((8,)),
    ]
    out = pl.pallas_call(
        kernel,
        out_shape=pltpu.VMEM((narrow, LANES), F32),
        in_specs=[pl.BlockSpec(memory_space=pl.ANY)] * 10,
        out_specs=pl.BlockSpec(memory_space=pltpu.VMEM),
        scratch_shapes=scratch,
        compiler_params=pltpu.CompilerParams(
            collective_id=0, has_side_effects=True, vmem_limit_bytes=60 * 1024 * 1024
        ),
    )(*flat)
    return out.reshape(NV, NK, CELLS, LANES)


def solution(mesh):
    grid = P(None, None, "chord", "span")
    deep = P(None, None, None, "chord", "span")
    return jax.shard_map(
        on_device,
        mesh=mesh,
        in_specs=(grid, deep, deep, deep, grid, grid, grid, grid, grid, grid),
        out_specs=grid,
        check_vma=False,
    )
```

```python
import functools

import jax
import jax.numpy as jnp
from jax import lax
from jax.experimental import pallas as pl
from jax.experimental.pallas import tpu as pltpu
from jax.sharding import PartitionSpec as P

F32 = jnp.float32
MESH = pl.DeviceIdType.MESH

NV = 5
NK = 4
CHORD = 32
SPAN = 8
CELLS = 32
LANES = 128
HALF = 16
GROUPS = 11
MAT, VEC, OUT, INN, SRC = 0, 25, 30, 55, 80
ZS, XS = 8, 4
WIDE = NV * NV * 128


def ring(step, size):
    return min(step, size - step)


CHORD_PEERS = sorted(
    [(dz, dx) for dz in range(ZS) for dx in range(XS) if dz or dx], key=lambda p: -ring(p[0], ZS) - ring(p[1], XS)
)
SPAN_PEERS = (4, 5, 3, 2, 6, 7, 1)


def dot(lhs, rhs):
    terms = [a * b for a, b in zip(lhs, rhs)]
    while len(terms) > 1:
        terms = [terms[i] + terms[i + 1] if i + 1 < len(terms) else terms[i] for i in range(0, len(terms), 2)]
    return terms[0]


def affine(lhs, rhs, extra):
    a, b, c, d, e = [x * y for x, y in zip(lhs, rhs)]
    return ((a + b) + (c + d)) + (e + extra)


def residue(extra, lhs, rhs):
    a, b, c, d, e = [x * y for x, y in zip(lhs, rhs)]
    return (extra - e) - ((a + b) + (c + d))


def column(matrix, index):
    return [row[index] for row in matrix]


def matmul(lhs, rhs):
    cols = [column(rhs, j) for j in range(len(rhs[0]))]
    return [[dot(row, col) for col in cols] for row in lhs]


def matvec(lhs, vec):
    return [dot(row, vec) for row in lhs]


def skewed_transpose(tile, blk):
    tile = pltpu.roll(tile, 0, 1, stride=16, stride_axis=0)
    for d in (1, 2, 4):
        tile = jnp.where((blk & d) != 0, pltpu.roll(tile, 8 - d, 0), tile)
    return pltpu.roll(tile, 0, 1, stride=16, stride_axis=0)


def kernel(
    res_h, piv_h, low_h, upp_h, sp_h, sl_h, su_h, np_h, nl_h, nu_h,
    out_ref,
    res, low, pair, spn, sln, sun, npn, nln, nun,
    lowf, pairf, prefix, source, state, comb, send1, recv1, expand, expand2, entry, entry2, total,
    send2, recv2, unsh, carry, ysweep, wnat,
    wt, pt, lt, ut, gain, pre, alp, bet, cc, aa,
    gsend, grecv, hsend, hrecv, sentry,
    wvar, alp_v, bet_v,
    load_sem, sems,
):
    me_c = lax.axis_index("chord")
    me_s = lax.axis_index("span")

    z, x = me_c // XS, lax.rem(me_c, XS)

    def chord_peer(peer):
        return lax.rem(z + peer[0], ZS) * XS + lax.rem(x + peer[1], XS)

    loads = {}
    for n, src, dst in [
        (2, low_h, low), (1, piv_h, pair.at[pl.ds(0, WIDE)]), (3, upp_h, pair.at[pl.ds(WIDE, WIDE)]),
        (0, res_h, res), (4, sp_h, spn), (5, sl_h, sln),
        (6, su_h, sun), (7, np_h, npn), (8, nl_h, nln), (9, nu_h, nun),
    ]:
        loads[n] = pltpu.make_async_copy(src, dst, load_sem.at[n])
    for n in (2, 1, 3, 0):
        loads[n].start()

    barrier = pltpu.get_barrier_semaphore()
    for peer in CHORD_PEERS:
        pl.semaphore_signal(barrier, inc=1, device_id={"chord": chord_peer(peer)}, device_id_type=MESH)
    for o in SPAN_PEERS:
        pl.semaphore_signal(barrier, inc=1, device_id={"span": lax.rem(me_s + o, SPAN)}, device_id_type=MESH)
    for n in range(4, 10):
        loads[n].start()

    lane = lax.broadcasted_iota(jnp.int32, (8, LANES), 1)
    blk = lane // 16

    to_row = lax.broadcasted_iota(jnp.int32, (LANES, LANES), 0)
    from_row = lax.broadcasted_iota(jnp.int32, (LANES, LANES), 1)
    order = jnp.where(from_row == HALF * lax.rem(to_row, 8) + to_row // 8, 1.0, 0.0).astype(jnp.bfloat16)

    def widen(src, dst, n):
        rows = pl.ds(pl.multiple_of(n * 128, 128), 128)
        dst[rows] = jnp.dot(order, src[rows], preferred_element_type=F32)

    loads[2].wait()
    for n in range(NV):
        rows = [pl.ds(128 * (NV * n + c), 128) for c in range(NV)]
        abreast = jnp.dot(order, jnp.concatenate([low[at] for at in rows], axis=1), preferred_element_type=F32)
        for c in range(NV):
            lowf[rows[c]] = abreast[:, 128 * c : 128 * c + 128]

    zero = jnp.zeros((8, LANES), F32)

    def tile_of(value):
        return pl.ds(8 * value, 8)

    def strided(ref, index, step):
        return ref[pl.ds(index * 128 + step, 8, stride=HALF)]

    def block(ref, index, step):
        return ref[pl.ds(pl.multiple_of(index * 128 + 8 * step, 8), 8)]

    def blocks(ref, step):
        return [[block(ref, 5 * r + c, step) for c in range(NV)] for r in range(NV)]

    def ahead_step(step):
        lows = blocks(lowf, step)
        for c in range(NV):
            new = matvec(lows, [state[tile_of(MAT + 5 * r + c)] for r in range(NV)])
            for r in range(NV):
                state[tile_of(MAT + 5 * r + c)] = new[r]
                prefix[pl.ds(pl.multiple_of((5 * r + c) * 128 + 8 * step, 8), 8)] = new[r]

    for index in range(NV * NV):
        low_0 = block(lowf, index, 0)
        state[tile_of(MAT + index)] = low_0
        prefix[pl.ds(index * 128, 8)] = low_0
    loads[1].wait()
    loads[3].wait()

    def ahead_steps(n, _):
        for t in range(3):
            ahead_step(3 * n + t + 1)
        for t in range(10):
            widen(pair, pairf, 10 * n + t)
        return 0

    lax.fori_loop(0, 5, ahead_steps, 0)
    loads[0].wait()

    def sources(step):
        cells = [strided(res, c, step) for c in range(NV)]
        src = [dot([block(pairf, 5 * r + c, step) for c in range(NV)], cells) for r in range(NV)]
        for r in range(NV):
            source[pl.ds(pl.multiple_of((step * NV + r) * 8, 8), 8)] = src[r]
        return src

    def upper(index, step):
        return block(pairf, NV * NV + index, step)

    def back_step(step, odd):
        src = sources(step)
        lows = blocks(lowf, step)
        vec = [state[tile_of(VEC + r)] for r in range(NV)]
        new = [affine(lows[r], vec, src[r]) if odd else -residue(src[r], lows[r], vec) for r in range(NV)]
        for r in range(NV):
            state[tile_of(VEC + r)] = new[r]
        mats = blocks(prefix, step)
        for r in range(NV):
            row = [state[tile_of(OUT + 5 * r + c)] for c in range(NV)]
            for c in range(NV):
                at = tile_of(INN + 5 * r + c)
                state[at] = affine(row, column(mats, c), state[at])
            at = tile_of(SRC + r)
            state[at] = affine(row, new, state[at])
        upps = [[upper(5 * r + c, step) for c in range(NV)] for r in range(NV)]
        for r in range(NV):
            row = [state[tile_of(OUT + 5 * r + c)] for c in range(NV)]
            for c in range(NV):
                state[tile_of(OUT + 5 * r + c)] = dot(row, column(upps, c))

    first = sources(0)
    for r in range(NV):
        for c in range(NV):
            state[tile_of(INN + 5 * r + c)] = block(lowf, 5 * r + c, 0)
            state[tile_of(OUT + 5 * r + c)] = upper(5 * r + c, 0)
        state[tile_of(VEC + r)] = -first[r]
        state[tile_of(SRC + r)] = -first[r]
    back_step(1, True)

    def back_pair(n, _):
        back_step(2 * n, False)
        back_step(2 * n + 1, True)
        return 0

    lax.fori_loop(1, HALF // 2, back_pair, 0)

    def half(value, which):
        return state[pl.ds(8 * value + which, NK, stride=2)]

    def half_matrix(base, which):
        return [[half(base + 5 * r + c, which) for c in range(NV)] for r in range(NV)]

    def half_vector(base, which):
        return [half(base + r, which) for r in range(NV)]

    def put(value, data):
        comb[pl.ds(NK * value, NK)] = data

    mat0 = half_matrix(MAT, 0)
    vec0 = half_vector(VEC, 0)
    mat1 = half_matrix(MAT, 1)
    mats = matmul(mat1, mat0)
    vecs = matvec(mat1, vec0)
    for r in range(NV):
        for c in range(NV):
            put(MAT + 5 * r + c, mats[r][c])
        put(VEC + r, vecs[r] + half(VEC + r, 1))
    inn1 = half_matrix(INN, 1)
    part = matmul(inn1, mat0)
    tail = [t + half(SRC + r, 1) for r, t in enumerate(matvec(inn1, vec0))]
    out0 = half_matrix(OUT, 0)
    outs = matmul(out0, half_matrix(OUT, 1))
    inns = matmul(out0, part)
    srcs = matvec(out0, tail)
    for r in range(NV):
        for c in range(NV):
            put(OUT + 5 * r + c, outs[r][c])
            put(INN + 5 * r + c, inns[r][c] + half(INN + 5 * r + c, 0))
        put(SRC + r, srcs[r] + half(SRC + r, 0))
    for value in range(85, 88):
        put(value, jnp.zeros((NK, LANES), F32))

    def shuffle(k):
        for g in range(GROUPS):
            tile = comb[pl.ds(NK * 8 * g + k, 8, stride=NK)]
            send1[pl.ds(8 * GROUPS * k + g, 8, stride=GROUPS), 0] = skewed_transpose(tile, blk)

    for k in range(NK):
        shuffle(k)

    pl.semaphore_wait(barrier, CHORD - 1 + SPAN - 1)

    def exchange(send, recv, rows, at, slot):
        for peer in CHORD_PEERS:
            to = chord_peer(peer)
            pltpu.make_async_remote_copy(
                src_ref=send.at[pl.ds(to * rows, rows)],
                dst_ref=recv.at[pl.ds(slot * rows, rows)],
                send_sem=sems.at[2 * at],
                recv_sem=sems.at[2 * at + 1],
                device_id={"chord": to},
                device_id_type=MESH,
            ).start()
        recv[pl.ds(slot * rows, rows)] = send[pl.ds(me_c * rows, rows)]

    def spread(send, recv, rows, at):
        for o in SPAN_PEERS:
            pltpu.make_async_remote_copy(
                src_ref=send,
                dst_ref=recv.at[pl.ds(me_s * rows, rows)],
                send_sem=sems.at[2 * at],
                recv_sem=sems.at[2 * at + 1],
                device_id={"span": lax.rem(me_s + o, SPAN)},
                device_id_type=MESH,
            ).start()
        recv[pl.ds(me_s * rows, rows)] = send[...]

    def settle(ref, rows, sem):
        whole = ref.at[pl.ds(0, rows)]
        pltpu.make_async_copy(whole, whole, sems.at[sem]).wait()

    exchange(send1, recv1, GROUPS, 0, me_c)

    for n, (src, dst) in enumerate([(spn, pt), (sln, lt), (sun, ut)]):
        loads[4 + n].wait()
        for v in range(NV):
            dst[pl.ds(v, LANES, stride=8)] = src[pl.ds(128 * v, 128)].T

    def at_j(j):
        return pl.ds(pl.multiple_of(8 * j, 8), NV)

    ones5 = jnp.ones((NV, LANES), F32)
    zeros5 = jnp.zeros((NV, LANES), F32)

    def gains_ahead(j, held):
        g, p = held
        g = -(lt[at_j(j)] * g)
        gain[at_j(j)] = g
        pre[at_j(j)] = p
        return (g, -(ut[at_j(j)] * p))

    g_end, _ = lax.fori_loop(0, LANES, gains_ahead, (ones5, ones5), unroll=8)

    def gains_back(n, held):
        suf, b, c, a, low_next = held
        j = LANES - 1 - n
        l, u, p = lt[at_j(j)], ut[at_j(j)], pt[at_j(j)]
        alp[at_j(j)] = suf * p
        b = pre[at_j(j)] - low_next * b
        bet[at_j(j)] = b * p
        c = -(u * c)
        cc[at_j(j)] = c
        a = gain[at_j(j)] - u * a
        aa[at_j(j)] = a
        return (-(l * suf), b, c, a, l)

    _, _, c_top, a_top, _ = lax.fori_loop(
        0, LANES, gains_back, (ones5, zeros5, ones5, zeros5, zeros5), unroll=8
    )
    gsend[pl.ds(0, NV), 0] = g_end
    gsend[pl.ds(NV, NV), 0] = a_top
    gsend[pl.ds(2 * NV, NV), 0] = c_top
    spread(gsend, grecv, 3 * NV, 2)
    for v in range(NV):
        alp_v[pl.ds(128 * v, 128)] = alp[pl.ds(v, LANES, stride=8)]
        bet_v[pl.ds(128 * v, 128)] = bet[pl.ds(v, LANES, stride=8)]

    settle(recv1, (CHORD - 1) * GROUPS, 1)

    ahead_values = 8 * (OUT // 8 + 1)

    def unpack(q, groups):
        for g in groups:
            tile = recv1[pl.ds(8 * GROUPS * q + g, 8, stride=GROUPS), 0]
            for s in range(8):
                value = 8 * g + s
                if value < 85:
                    moved = tile if s == 0 else pltpu.roll(tile, LANES - 16 * s, 1)
                    if value < ahead_values:
                        expand[pl.ds(pl.multiple_of(CHORD * value + 8 * q, 8), 8)] = moved
                    if value >= OUT:
                        expand2[pl.ds(pl.multiple_of(CHORD * (value - OUT) + 8 * q, 8), 8)] = moved

    def row(value, at):
        return expand[pl.ds(CHORD * value + at, 1)]

    def row2(value, at):
        return expand2[pl.ds(CHORD * (value - OUT) + at, 1)]

    def tile2(value, q):
        return expand2[pl.ds(pl.multiple_of(CHORD * (value - OUT) + 8 * q, 8), 8)]

    def relay_ahead(q, held):
        for n in range(8):
            at = 8 * q + n
            new = []
            for c in range(NV):
                entry[pl.ds(CHORD * c + at, 1)] = held[c]
            for r in range(NV):
                new.append(affine([row(MAT + 5 * r + c, at) for c in range(NV)], held, row(VEC + r, at)))
            held = new
        return held

    held = [jnp.zeros((1, LANES), F32) for _ in range(NV)]
    for q in range(CHORD // 8):
        unpack(q, range(ahead_values // 8))
    for q in range(CHORD // 8):
        held = relay_ahead(q, held)
        unpack(q, range(ahead_values // 8, GROUPS))

    for q in range(CHORD // 8):
        vec = [entry[pl.ds(CHORD * c + 8 * q, 8)] for c in range(NV)]
        for r in range(NV):
            mats_r = [tile2(INN + 5 * r + c, q) for c in range(NV)]
            total[pl.ds(CHORD * r + 8 * q, 8)] = -affine(mats_r, vec, tile2(SRC + r, q))

    def relay_back(q, held):
        for n in reversed(range(8)):
            at = 8 * q + n
            new = []
            for c in range(NV):
                entry2[pl.ds(CHORD * c + at, 1)] = held[c]
            for r in range(NV):
                new.append(
                    affine([row2(OUT + 5 * r + c, at) for c in range(NV)], held, total[pl.ds(CHORD * r + at, 1)])
                )
            held = new
        return held

    held = [jnp.zeros((1, LANES), F32) for _ in range(NV)]
    for q in reversed(range(CHORD // 8)):
        held = relay_back(q, held)

    for q in range(CHORD // 8):
        for kind in range(2):
            tile = zero
            for s in range(NV):
                part_s = (entry2 if kind else entry)[pl.ds(CHORD * s + 8 * q, 8)]
                if s > 0:
                    part_s = pltpu.roll(part_s, 16 * s, 1)
                tile = jnp.where(blk == s, part_s, tile)
            send2[pl.ds(16 * q + kind, 8, stride=2), 0] = tile

    exchange(send2, recv2, 2, 1, me_c // 8 * 8 + lax.rem(8 - lax.rem(me_c, 8), 8))

    settle(recv2, (CHORD - 1) * 2, 3)

    for kind in range(2):
        for k in range(NK):
            tile = recv2[pl.ds(16 * k + kind, 8, stride=2), 0]
            unsh[pl.ds(8 * (NK * kind + k), 8)] = skewed_transpose(tile, blk)
    a0 = [unsh[pl.ds((8 - v) % 8, NK, stride=8)] for v in range(NV)]
    c1 = [unsh[pl.ds(8 * NK + (8 - v) % 8, NK, stride=8)] for v in range(NV)]
    a1 = [m + half(VEC + r, 0) for r, m in enumerate(matvec(half_matrix(MAT, 0), a0))]
    back = matvec(half_matrix(OUT, 1), c1)
    fore = matvec(half_matrix(INN, 1), a1)
    c0 = [back[r] - (fore[r] + half(SRC + r, 1)) for r in range(NV)]
    for v in range(NV):
        carry[pl.ds(8 * v, NK, stride=2)] = a0[v]
        carry[pl.ds(8 * v + 1, NK, stride=2)] = a1[v]
        carry[pl.ds(8 * (NV + v), NK, stride=2)] = c0[v]
        carry[pl.ds(8 * (NV + v) + 1, NK, stride=2)] = c1[v]

    def by_step(ref, step, r):
        return [block(ref, NV * r + c, step) for c in range(NV)]

    def sweep_ahead(step, held):
        new = []
        for r in range(NV):
            at = pl.ds(pl.multiple_of((step * NV + r) * 8, 8), 8)
            val = residue(source[at], by_step(lowf, step, r), held)
            ysweep[at] = val
            new.append(val)
        return tuple(new)

    lax.fori_loop(0, HALF, sweep_ahead, tuple(carry[tile_of(v)] for v in range(NV)), unroll=16)

    def sweep_back(n, held):
        step = HALF - 1 - n
        new = []
        for r in range(NV):
            at = pl.ds(pl.multiple_of((step * NV + r) * 8, 8), 8)
            val = residue(ysweep[at], by_step(pairf, step, r + NV), held)
            wnat[pl.ds(128 * r + step, 8, stride=HALF)] = val
            new.append(val)
        return tuple(new)

    lax.fori_loop(0, HALF, sweep_back, tuple(carry[tile_of(NV + v)] for v in range(NV)), unroll=16)

    for v in range(NV):
        turned = wnat[pl.ds(128 * v, 128)].T
        wvar[pl.ds(128 * v, 128)] = turned
        for kind, weight in enumerate((alp_v, bet_v)):
            terms = [turned[8 * t : 8 * t + 8] * weight[pl.ds(128 * v + 8 * t, 8)] for t in range(16)]
            while len(terms) > 1:
                terms = [terms[t] + terms[t + 1] for t in range(0, len(terms), 2)]
            hsend[pl.ds(NV * kind + v, 1), 0] = jnp.sum(terms[0], axis=0, keepdims=True)
    spread(hsend, hrecv, 2 * NV, 3)
    for v in range(NV):
        wt[pl.ds(v, LANES, stride=8)] = wvar[pl.ds(128 * v, 128)]

    def span_ahead(j, z):
        z = pt[at_j(j)] * wt[at_j(j)] - lt[at_j(j)] * z
        wt[at_j(j)] = z
        return z

    lax.fori_loop(0, LANES, span_ahead, zeros5, unroll=8)

    def span_back(n, z):
        j = LANES - 1 - n
        z = wt[at_j(j)] - ut[at_j(j)] * z
        wt[at_j(j)] = z
        return z

    lax.fori_loop(0, LANES, span_back, zeros5, unroll=8)

    settle(grecv, (SPAN - 1) * 3 * NV, 5)
    settle(hrecv, (SPAN - 1) * 2 * NV, 7)
    a = zeros5
    sent = []
    for d in range(SPAN):
        sentry[pl.ds(8 * d, NV)] = a
        sent.append(a)
        a = hrecv[pl.ds(2 * NV * d, NV), 0] + grecv[pl.ds(3 * NV * d, NV), 0] * a
    c = zeros5
    for d in reversed(range(SPAN)):
        sentry[pl.ds(8 * (SPAN + d), NV)] = c
        c = (
            hrecv[pl.ds(2 * NV * d + NV, NV), 0]
            + grecv[pl.ds(3 * NV * d + NV, NV), 0] * sent[d]
            + grecv[pl.ds(3 * NV * d + 2 * NV, NV), 0] * c
        )
    a_in = sentry[pl.ds(pl.multiple_of(8 * me_s, 8), NV)]
    c_in = sentry[pl.ds(pl.multiple_of(8 * (SPAN + me_s), 8), NV)]

    def close(j, _):
        wt[at_j(j)] = wt[at_j(j)] + aa[at_j(j)] * a_in + cc[at_j(j)] * c_in
        return 0

    lax.fori_loop(0, LANES, close, 0, unroll=32)

    for n in range(7, 10):
        loads[n].wait()
    for v in range(NV):
        x = wt[pl.ds(v, LANES, stride=8)].T
        held = None
        planes = []
        for k in range(NK):
            at = pl.ds(128 * v + 32 * k, 32)
            now = npn[at].astype(F32) * x[32 * k : 32 * k + 32]
            held = now if held is None else now - nln[at].astype(F32) * held
            planes.append(held)
        held = None
        for k in reversed(range(NK)):
            at = pl.ds(128 * v + 32 * k, 32)
            held = planes[k] if held is None else planes[k] - nun[at].astype(F32) * held
            out_ref[at] = held

    settle(send1, (CHORD - 1) * GROUPS, 0)
    settle(send2, (CHORD - 1) * 2, 2)
    settle(grecv, (SPAN - 1) * 3 * NV, 4)
    settle(hrecv, (SPAN - 1) * 2 * NV, 6)


def on_device(*args):
    flat = [a.reshape(-1, LANES) for a in args]
    f32 = lambda *shape: pltpu.VMEM(shape, F32)
    b16 = lambda *shape: pltpu.VMEM(shape, jnp.bfloat16)
    wide, narrow = NV * NV * 128, NV * 128
    scratch = [
        f32(narrow, LANES), b16(wide, LANES), b16(2 * wide, LANES),
        f32(narrow, LANES), f32(narrow, LANES), f32(narrow, LANES),
        b16(narrow, LANES), b16(narrow, LANES), b16(narrow, LANES),
        f32(wide, LANES), f32(2 * wide, LANES), f32(wide, LANES),
        f32(HALF * NV * 8, LANES),
        f32(88 * 8, LANES),
        f32(88 * NK, LANES),
        f32(CHORD * GROUPS, 1, LANES), f32(CHORD * GROUPS, 1, LANES),
        f32(32 * CHORD, LANES), f32(55 * CHORD, LANES),
        f32(NV * CHORD, LANES), f32(NV * CHORD, LANES), f32(NV * CHORD, LANES),
        f32(2 * CHORD, 1, LANES), f32(2 * CHORD, 1, LANES),
        f32(64, LANES), f32(80, LANES),
        f32(HALF * NV * 8, LANES), f32(narrow, LANES),
    ]
    scratch += [f32(8 * LANES, LANES) for _ in range(10)]
    scratch += [
        f32(3 * NV, 1, LANES), f32(SPAN * 3 * NV, 1, LANES),
        f32(2 * NV, 1, LANES), f32(SPAN * 2 * NV, 1, LANES),
        f32(2 * SPAN * 8, LANES),
        f32(narrow, LANES), f32(narrow, LANES), f32(narrow, LANES),
        pltpu.SemaphoreType.DMA((10,)),
        pltpu.SemaphoreType.DMA((8,)),
    ]
    out = pl.pallas_call(
        kernel,
        out_shape=pltpu.VMEM((narrow, LANES), F32),
        in_specs=[pl.BlockSpec(memory_space=pl.ANY)] * 10,
        out_specs=pl.BlockSpec(memory_space=pltpu.VMEM),
        scratch_shapes=scratch,
        compiler_params=pltpu.CompilerParams(
            collective_id=0, has_side_effects=True, vmem_limit_bytes=60 * 1024 * 1024
        ),
    )(*flat)
    return out.reshape(NV, NK, CELLS, LANES)


def solution(mesh):
    grid = P(None, None, "chord", "span")
    deep = P(None, None, None, "chord", "span")
    return jax.shard_map(
        on_device,
        mesh=mesh,
        in_specs=(grid, deep, deep, deep, grid, grid, grid, grid, grid, grid),
        out_specs=grid,
        check_vma=False,
    )
```
